512 devices in a mesh: layer: 8 (over x, y_lo), latent: 64 (over z, y_hi, core).
Axes of the slice: x: 4, y: 8 (y_hi: 4, y_lo: 2; y = y_hi * 2 + y_lo), z: 8, core: 2. Of those that a mesh axis runs over, the one named last changes fastest.
Arguments:
- residual: bfloat16 [512, 4608], P('latent', 'layer'), may hold values from -6 to 6
- w_enc: bfloat16 [4608, 65536], P('layer', 'latent'), may hold values from -0.09375 to 0.09375
- b_enc: float32 [65536], P('latent'), may hold values from -1 to 0.5
- w_dec: bfloat16 [65536, 4608], P('latent', 'layer'), may hold values from -0.0234375 to 0.0234375
- b_dec: float32 [4608], P('layer'), may hold values from -3 to 3
Outputs:
- grad_enc: bfloat16 [4608, 65536], P('layer', 'latent')
- grad_benc: bfloat16 [65536], P('latent')
- grad_dec: bfloat16 [65536, 4608], P('latent', 'layer')
- grad_bdec: bfloat16 [4608], P('layer')
- loss: float32 [], replicated
The draws below stay inside these ranges and needn't reach their ends.
All inputs are finite; a program needn't handle non-finite values.
Results may differ from the reference program's by a relative error of at most 0.02.
Values may be sent and summed in bfloat16 or wider, within the bound.
No kernel may reach another device: no remote copies, remote signals or barrier semaphores. Data moves between devices by JAX's collectives and lax.ppermute only.
A program may use at most 64 MiB of HBM per device.

```python
import jax
import jax.numpy as jnp
from jax import lax

D = 4608
LATENTS = 65536
ROWS = 512


def block_scale(stream_key, extent, pieces, least, largest):
    factor_of = 1.0
    for axis_at, parts in pieces:
        draws = jax.random.uniform(jax.random.fold_in(jax.random.fold_in(stream_key, 6), axis_at), (parts,), jnp.float32, least / len(pieces), largest / len(pieces))
        factor_of = factor_of * jnp.repeat(jnp.exp(draws), extent[axis_at] // parts).reshape((-1,) + (1,) * (len(extent) - 1 - axis_at))
    return factor_of


def bell_draw(own_key, dims, scale, most, pieces=(), dtype=jnp.bfloat16):
    drawn = scale * jax.random.normal(own_key, dims, jnp.float32)
    if pieces:
        drawn = drawn * block_scale(own_key, dims, pieces, -0.22, 0.18)
    return jnp.clip(drawn, -most, most).astype(dtype)


def setup_inputs(seed: int = 0) -> dict:
    arg_keys = jax.random.split(jax.random.key(seed), 6)
    residual = bell_draw(arg_keys[0], (ROWS, D), 1.0, 6.0, ((0, 64), (1, 8)))
    w_enc = bell_draw(arg_keys[1], (D, LATENTS), D ** -0.5, 0.09375, ((0, 8), (1, 64)))
    b_enc = jnp.clip(-1.0 + 1.5 * jax.random.uniform(arg_keys[2], (LATENTS,), jnp.float32) ** block_scale(arg_keys[2], (LATENTS,), ((0, 64),), -0.2, 0.2), -1.0, 0.5)
    w_dec = bell_draw(arg_keys[3], (LATENTS, D), LATENTS ** -0.5, 0.0234375, ((0, 64), (1, 8)))
    b_dec = bell_draw(arg_keys[4], (D,), 0.5, 3.0, ((0, 8),), jnp.float32)
    return {"residual": residual, "w_enc": w_enc, "b_enc": b_enc, "w_dec": w_dec, "b_dec": b_dec}


penalty_weight = 0.5

def reference(residual, w_enc, b_enc, w_dec, b_dec):
    pre = jnp.dot(residual, w_enc, preferred_element_type=jnp.float32) + b_enc
    acts = jnp.maximum(pre, 0.0).astype(jnp.bfloat16)
    wide = w_dec.astype(jnp.float32)
    norms = jnp.sqrt(lax.optimization_barrier(jnp.sum(wide * wide, axis=1)) + 1e-06)
    recon = jnp.dot(acts, w_dec, preferred_element_type=jnp.float32) + b_dec
    err = recon - residual.astype(jnp.float32)
    acts_wide = acts.astype(jnp.float32)
    total = jnp.sum(err * err) + penalty_weight * jnp.sum(acts_wide * norms[None, :])
    loss = total / (ROWS * D)
    d_recon = (err / 8.0).astype(jnp.bfloat16)
    grad_bdec = lax.optimization_barrier(jnp.sum(d_recon.astype(jnp.float32), axis=0)).astype(jnp.bfloat16)
    col_sum = lax.optimization_barrier(jnp.sum(acts_wide, axis=0))
    outer = lax.dot_general(acts, d_recon, (((0,), (0,)), ((), ())), preferred_element_type=jnp.float32)
    grad_dec = (outer + penalty_weight / 16.0 * col_sum[:, None] * wide / norms[:, None]).astype(jnp.bfloat16)
    d_acts = lax.dot_general(d_recon, w_dec, (((1,), (1,)), ((), ())), preferred_element_type=jnp.float32)
    d_acts = d_acts + penalty_weight / 16.0 * norms[None, :]
    d_pre = jnp.where(acts > 0, d_acts, 0.0).astype(jnp.bfloat16)
    grad_enc = lax.dot_general(residual, d_pre, (((0,), (0,)), ((), ())), preferred_element_type=jnp.float32).astype(jnp.bfloat16)
    grad_benc = lax.optimization_barrier(jnp.sum(d_pre.astype(jnp.float32), axis=0)).astype(jnp.bfloat16)
    return (grad_enc, grad_benc, grad_dec, grad_bdec, loss)
```

```python
import jax
import jax.numpy as jnp
from jax import lax
from jax.sharding import Mesh, PartitionSpec as P

D = 4608
ROWS = 512
LAYER = ("x", "yl")
CHIPS = ("z", "yh")
LATENT = ("z", "yh", "c")
f32, bf16 = jnp.float32, jnp.bfloat16

penalty_weight = 0.5


def exchange(blocks, axes):
    return lax.all_to_all(blocks, axes, 0, 0, tiled=True)


def spread(block, axes, count):
    return exchange(jnp.broadcast_to(block[None], (count,) + block.shape), axes)


def split(value):
    high = lax.reduce_precision(value, exponent_bits=8, mantissa_bits=7)
    return high.astype(bf16), (value - high).astype(bf16)


def chunked(value):
    return value.reshape(8, 64, 8, 128).transpose(0, 2, 1, 3).reshape(8, 512, 128)


def whole(value):
    return value.reshape(8, 8, 64, 128).transpose(0, 2, 1, 3).reshape(512, 1024)


def local(residual, w_enc, b_enc, w_dec, b_dec):
    core = lax.axis_index("c")
    near = spread(residual, CHIPS, 32).reshape(256, 576)
    rows_all = lax.all_gather(near, "c", axis=0, tiled=True)
    wide = w_dec.astype(f32)
    squares = jnp.stack(split(jnp.sum(wide * wide, axis=1).reshape(8, 128))).reshape(1, 16, 128)

    part = chunked(jnp.dot(rows_all, w_enc, preferred_element_type=f32))
    sent = jnp.concatenate([part.astype(bf16), jnp.broadcast_to(squares, (8, 16, 128))], axis=1)
    got = jnp.sum(exchange(sent, LAYER).astype(f32), axis=0)
    bias = b_enc.reshape(8, 1, 128)
    norms = jnp.sqrt(got[512:520] + got[520:528] + 1e-06)
    acts_own = jnp.maximum(got[:512].reshape(8, 64, 128) + bias, 0.0).astype(bf16)
    penalty_part = penalty_weight * jnp.sum(acts_own.astype(f32) * norms[:, None, :])
    acts = whole(spread(acts_own.reshape(512, 128), LAYER, 8))
    exact = lax.psum_scatter(part, LAYER, scatter_dimension=0, tiled=True)
    active = exact.reshape(8, 64, 128) + bias > 0

    recon_part = jnp.dot(acts, w_dec, preferred_element_type=f32).reshape(2, 256, 576)
    other = lax.dynamic_index_in_dim(recon_part, 1 - core, 0, keepdims=False).astype(bf16)
    mine = lax.dynamic_index_in_dim(recon_part, core, 0, keepdims=False)
    pair = mine + lax.ppermute(other, "c", [(0, 1), (1, 0)]).astype(f32)
    recon = jnp.sum(exchange(pair.astype(bf16).reshape(32, 8, 576), CHIPS).astype(f32), axis=0) + b_dec
    err = recon - residual.astype(f32)
    high, low = split(jnp.sum(err * err) + penalty_part)
    column = lax.broadcasted_iota(jnp.int32, (8, 64), 1)
    row = lax.broadcasted_iota(jnp.int32, (8, 64), 0)
    tail = jnp.where((row == 0) & (column == 0), high, jnp.where((row == 0) & (column == 1), low, jnp.zeros((), bf16)))
    packed = jnp.concatenate([(err / 8.0).astype(bf16), tail], axis=1)
    packed = spread(packed, CHIPS, 32).reshape(256, 640)
    packed = lax.all_gather(packed, "c", axis=0, tiled=True)
    d_recon = packed[:, :576]
    total = jnp.sum(packed[:, 576:].astype(f32))
    high, low = split(total)
    at = lax.broadcasted_iota(jnp.int32, (16, 128), 1)
    up = lax.broadcasted_iota(jnp.int32, (16, 128), 0)
    tail = jnp.where((up == 0) & (at == 0), high, jnp.where((up == 0) & (at == 1), low, jnp.zeros((), bf16)))

    act_part = lax.dot_general(d_recon, w_dec, (((1,), (1,)), ((), ())), preferred_element_type=f32)
    sent = jnp.concatenate([chunked(act_part).astype(bf16), jnp.broadcast_to(tail[None], (8, 16, 128))], axis=1)
    got = jnp.sum(exchange(sent, LAYER).astype(f32), axis=0)
    loss = jnp.sum(got[512:]) / (ROWS * D)
    d_acts = got[:512].reshape(8, 64, 128) + penalty_weight / 16.0 * norms[:, None, :]
    d_pre_own = jnp.where(active, d_acts, 0.0).astype(bf16).reshape(512, 128)

    grad_bdec = jnp.sum(d_recon.astype(f32), axis=0).astype(bf16)
    col_sum = jnp.sum(acts.astype(f32), axis=0)
    outer = lax.dot_general(acts, d_recon, (((0,), (0,)), ((), ())), preferred_element_type=f32)
    scale = penalty_weight / 16.0 * col_sum / norms.reshape(1024)
    grad_dec = (outer + scale[:, None] * wide).astype(bf16)

    d_pre = whole(spread(d_pre_own, LAYER, 8))
    grad_enc = lax.dot_general(rows_all, d_pre, (((0,), (0,)), ((), ())), preferred_element_type=f32).astype(bf16)
    grad_benc = jnp.sum(d_pre.astype(f32), axis=0).astype(bf16)
    return (grad_enc, grad_benc, grad_dec, grad_bdec, loss)


def solution(mesh):
    fine = Mesh(mesh.devices.reshape(4, 2, 8, 4, 2), ("x", "yl", "z", "yh", "c"))
    placed = (P(LATENT, LAYER), P(LAYER, LATENT), P(LATENT), P(LATENT, LAYER), P(LAYER))
    return jax.shard_map(
        local,
        mesh=fine,
        in_specs=placed,
        out_specs=(P(LAYER, LATENT), P(LATENT), P(LATENT, LAYER), P(LAYER), P()),
        check_vma=False,
    )
```

```python
import jax
import jax.numpy as jnp
from jax import lax
from jax.sharding import Mesh, PartitionSpec as P

D = 4608
ROWS = 512
LAYER = ("x", "yl")
CHIPS = ("z", "yh")
LATENT = ("z", "yh", "c")
f32, bf16 = jnp.float32, jnp.bfloat16

penalty_weight = 0.5


def exchange(blocks, axes):
    return lax.all_to_all(blocks, axes, 0, 0, tiled=True)


def spread(block, axes, count):
    return exchange(jnp.broadcast_to(block[None], (count,) + block.shape), axes)


def split(value):
    high = lax.reduce_precision(value, exponent_bits=8, mantissa_bits=7)
    return high.astype(bf16), (value - high).astype(bf16)


def forward(block, by):
    pairs = [(x * 2 + y, (x + by[0]) % 4 * 2 + (y + by[1]) % 2) for x in range(4) for y in range(2)]
    return lax.ppermute(block, LAYER, pairs)


def remainders(low, steps):
    at_x, at_y = lax.axis_index("x"), lax.axis_index("yl")
    total = None
    for by in steps:
        to = (at_x + by[0]) % 4 * 2 + (at_y + by[1]) % 2
        block = lax.dynamic_index_in_dim(low, to, 0, keepdims=False)
        block = (block if by == (0, 0) else forward(block, by)).astype(f32)
        total = block if total is None else total + block
    return total


def chunked(value):
    return value.reshape(8, 64, 8, 128).transpose(0, 2, 1, 3).reshape(8, 512, 128)


def whole(value):
    return value.reshape(8, 8, 64, 128).transpose(0, 2, 1, 3).reshape(512, 1024)


def local(residual, w_enc, b_enc, w_dec, b_dec):
    core = lax.axis_index("c")
    near = spread(residual, CHIPS, 32).reshape(256, 576)
    rows_all = lax.all_gather(near, "c", axis=0, tiled=True)
    wide = w_dec.astype(f32)
    squares = jnp.stack(split(jnp.sum(wide * wide, axis=1).reshape(8, 128))).reshape(1, 16, 128)

    part = chunked(jnp.dot(rows_all, w_enc, preferred_element_type=f32))
    sent = jnp.concatenate([part.astype(bf16), jnp.broadcast_to(squares, (8, 16, 128))], axis=1)
    pre = jnp.sum(exchange(sent, LAYER).astype(f32), axis=0)
    bias = b_enc.reshape(8, 1, 128)
    norms = jnp.sqrt(pre[512:520] + pre[520:528] + 1e-06)
    acts_own = jnp.maximum(pre[:512].reshape(8, 64, 128) + bias, 0.0).astype(bf16)
    penalty_part = penalty_weight * jnp.sum(acts_own.astype(f32) * norms[:, None, :])
    acts = whole(spread(acts_own.reshape(512, 128), LAYER, 8))
    _, low_part = split(part)

    recon_part = jnp.dot(acts, w_dec, preferred_element_type=f32).reshape(2, 256, 576)
    other = lax.dynamic_index_in_dim(recon_part, 1 - core, 0, keepdims=False).astype(bf16)
    mine = lax.dynamic_index_in_dim(recon_part, core, 0, keepdims=False)
    pair = mine + lax.ppermute(other, "c", [(0, 1), (1, 0)]).astype(f32)
    pair, low_part = lax.optimization_barrier((pair, low_part))
    fine = remainders(low_part, [(0, 0), (0, 1), (1, 0), (1, 1)])
    recon, fine = lax.optimization_barrier((exchange(pair.astype(bf16).reshape(32, 8, 576), CHIPS), fine))
    recon = jnp.sum(recon.astype(f32), axis=0) + b_dec
    err = recon - residual.astype(f32)
    high, low = split(jnp.sum(err * err) + penalty_part)
    column = lax.broadcasted_iota(jnp.int32, (8, 64), 1)
    row = lax.broadcasted_iota(jnp.int32, (8, 64), 0)
    tail = jnp.where((row == 0) & (column == 0), high, jnp.where((row == 0) & (column == 1), low, jnp.zeros((), bf16)))
    packed = jnp.concatenate([(err / 8.0).astype(bf16), tail], axis=1)
    packed, low_part = lax.optimization_barrier((packed, low_part))
    fine = fine + remainders(low_part, [(2, 0), (2, 1), (3, 0), (3, 1)])
    packed, fine = lax.optimization_barrier((spread(packed, CHIPS, 32), fine))
    packed = packed.reshape(256, 640)
    packed = lax.all_gather(packed, "c", axis=0, tiled=True)
    d_recon = packed[:, :576]
    total = jnp.sum(packed[:, 576:].astype(f32))
    high, low = split(total)
    at = lax.broadcasted_iota(jnp.int32, (16, 128), 1)
    up = lax.broadcasted_iota(jnp.int32, (16, 128), 0)
    tail = jnp.where((up == 0) & (at == 0), high, jnp.where((up == 0) & (at == 1), low, jnp.zeros((), bf16)))

    act_part = lax.dot_general(d_recon, w_dec, (((1,), (1,)), ((), ())), preferred_element_type=f32)
    sent = jnp.concatenate([chunked(act_part).astype(bf16), jnp.broadcast_to(tail[None], (8, 16, 128))], axis=1)
    got = jnp.sum(exchange(sent, LAYER).astype(f32), axis=0)
    loss = jnp.sum(got[512:]) / (ROWS * D)
    d_acts = got[:512].reshape(8, 64, 128) + penalty_weight / 16.0 * norms[:, None, :]
    active = (pre[:512] + fine).reshape(8, 64, 128) + bias > 0
    d_pre_own = jnp.where(active, d_acts, 0.0).astype(bf16).reshape(512, 128)

    grad_bdec = jnp.sum(d_recon.astype(f32), axis=0).astype(bf16)
    col_sum = jnp.sum(acts.astype(f32), axis=0)
    outer = lax.dot_general(acts, d_recon, (((0,), (0,)), ((), ())), preferred_element_type=f32)
    scale = penalty_weight / 16.0 * col_sum / norms.reshape(1024)
    grad_dec = (outer + scale[:, None] * wide).astype(bf16)

    d_pre = whole(spread(d_pre_own, LAYER, 8))
    grad_enc = lax.dot_general(rows_all, d_pre, (((0,), (0,)), ((), ())), preferred_element_type=f32).astype(bf16)
    grad_benc = jnp.sum(d_pre.astype(f32), axis=0).astype(bf16)
    return (grad_enc, grad_benc, grad_dec, grad_bdec, loss)


def solution(mesh):
    fine = Mesh(mesh.devices.reshape(4, 2, 8, 4, 2), ("x", "yl", "z", "yh", "c"))
    placed = (P(LATENT, LAYER), P(LAYER, LATENT), P(LATENT), P(LATENT, LAYER), P(LAYER))
    return jax.shard_map(
        local,
        mesh=fine,
        in_specs=placed,
        out_specs=(P(LAYER, LATENT), P(LATENT), P(LATENT, LAYER), P(LAYER), P()),
        check_vma=False,
    )
```

```python
import jax
import jax.numpy as jnp
from jax import lax
from jax.experimental import pallas as pl
from jax.experimental.pallas import tpu as pltpu
from jax.sharding import Mesh, PartitionSpec as P

D = 4608
ROWS = 512
LAYER = ("x", "yl")
CHIPS = ("z", "yh")
LATENT = ("z", "yh", "c")
f32, bf16 = jnp.float32, jnp.bfloat16

penalty_weight = 0.5


def call(body, outs, *args, flops=0, smem=()):
    outs = [jax.ShapeDtypeStruct(shape, dtype) for shape, dtype in outs]
    size = sum(a.size * a.dtype.itemsize for a in args) + sum(o.size * o.dtype.itemsize for o in outs)
    return pl.pallas_call(
        body,
        out_shape=outs,
        in_specs=[
            pl.BlockSpec(memory_space=pltpu.SMEM if i in smem else pltpu.VMEM) for i in range(len(args))
        ],
        out_specs=[pl.BlockSpec(memory_space=pltpu.VMEM) for _ in outs],
        cost_estimate=pl.CostEstimate(flops=flops, bytes_accessed=size, transcendentals=0),
        compiler_params=pltpu.CompilerParams(vmem_limit_bytes=24 * 2**20),
    )(*args)


def matmul(a, b, dims):
    return lax.dot_general(a, b, (dims, ((), ())), preferred_element_type=f32)


def row_block(ref, lo, count):
    parts = [ref[pl.ds(lo, count), q * 64 : (q + 1) * 64, :].reshape(count * 64, 128) for q in range(8)]
    return jnp.concatenate(parts, axis=1)


def encode(rows_ref, w_ref, squares_ref, sent_ref, low_ref):
    rows = rows_ref[...]
    for n in range(4):
        part = matmul(rows, w_ref[:, n * 256 : (n + 1) * 256], ((1,), (0,)))
        high = part.astype(bf16)
        low = (part - high.astype(f32)).astype(bf16)
        for h in range(2):
            at = pl.ds((2 * n + h) * 64, 64)
            sent_ref[:, at, :] = high[:, h * 128 : (h + 1) * 128].reshape(8, 64, 128)
            low_ref[:, at, :] = low[:, h * 128 : (h + 1) * 128].reshape(8, 64, 128)
    sent_ref[:, 512:528, :] = jnp.broadcast_to(squares_ref[...][None], (8, 16, 128))


def activate(got_ref, bias_ref, acts_ref, pre_ref, norms_ref, penalty_ref):
    extra = jnp.sum(got_ref[:, 512:528, :].astype(f32), axis=0)
    norms = jnp.sqrt(extra[:8] + extra[8:] + 1e-06)
    norms_ref[...] = norms
    penalty = jnp.zeros((1, 128), f32)
    for q in range(8):
        at = pl.ds(q * 64, 64)
        pre = jnp.sum(got_ref[:, at, :].astype(f32), axis=0) + bias_ref[q : q + 1, :]
        pre_ref[at, :] = pre
        acts = jnp.maximum(pre, 0.0).astype(bf16)
        acts_ref[:, at, :] = jnp.broadcast_to(acts[None], (8, 64, 128))
        penalty = penalty + jnp.sum(acts.astype(f32), axis=0, keepdims=True) * norms[q : q + 1, :]
    penalty_ref[...] = penalty_weight * penalty


def decode(half_ref, acts_ref, w_ref, out_ref):
    acts = row_block(acts_ref, half_ref[0] * 4, 4)
    out_ref[...] = matmul(acts, w_ref[...], ((1,), (1,))).astype(out_ref.dtype)


def residue(got_ref, bias_ref, residual_ref, penalty_ref, out_ref):
    recon = jnp.sum(got_ref[...].astype(f32).reshape(32, 8, 576), axis=0) + bias_ref[...]
    err = recon - residual_ref[...]
    total = jnp.sum(err * err, axis=(0, 1), keepdims=True) + jnp.sum(penalty_ref[...], axis=(0, 1), keepdims=True)
    high = total.astype(bf16).astype(f32)
    row = lax.broadcasted_iota(jnp.int32, (8, 64), 0)
    lane = lax.broadcasted_iota(jnp.int32, (8, 64), 1)
    tail = jnp.where(row == 0, jnp.where(lane == 0, high, jnp.where(lane == 1, total - high, 0.0)), 0.0)
    block = jnp.concatenate([err / 8.0, tail], axis=1)
    out_ref[...] = jnp.broadcast_to(block[None], (32, 8, 640)).reshape(256, 640).astype(bf16)


def decode_back(err_ref, w_ref, sent_ref):
    err = err_ref[:, :576]
    lane = lax.broadcasted_iota(jnp.int32, (512, 128), 1)
    tail = jnp.where(lane >= 64, err_ref[:, 512:640].astype(f32), 0.0)
    total = jnp.sum(tail, axis=(0, 1), keepdims=True)
    high = total.astype(bf16).astype(f32)
    row = lax.broadcasted_iota(jnp.int32, (16, 128), 0)
    lane = lax.broadcasted_iota(jnp.int32, (16, 128), 1)
    tail = jnp.where(row == 0, jnp.where(lane == 0, high, jnp.where(lane == 1, total - high, 0.0)), 0.0)
    sent_ref[:, 512:528, :] = jnp.broadcast_to(tail.astype(bf16)[None], (8, 16, 128))
    for n in range(4):
        part = matmul(err, w_ref[:, n * 256 : (n + 1) * 256], ((1,), (0,))).astype(bf16)
        for h in range(2):
            at = pl.ds((2 * n + h) * 64, 64)
            sent_ref[:, at, :] = part[:, h * 128 : (h + 1) * 128].reshape(8, 64, 128)


def mask(got_ref, pre_ref, fine_ref, norms_ref, out_ref, loss_ref):
    for q in range(8):
        at = pl.ds(q * 64, 64)
        d_acts = jnp.sum(got_ref[:, at, :].astype(f32), axis=0)
        d_acts = d_acts + penalty_weight / 16.0 * norms_ref[q : q + 1, :]
        d_pre = jnp.where(pre_ref[at, :] + fine_ref[at, :] > 0, d_acts, 0.0).astype(bf16)
        out_ref[:, at, :] = jnp.broadcast_to(d_pre[None], (8, 64, 128))
    total = jnp.sum(got_ref[:, 512:528, :].astype(f32), axis=0)
    loss_ref[...] = jnp.sum(total, axis=(0, 1), keepdims=True) / (ROWS * D)


def decoder_gradient(acts_ref, err_ref, w_ref, norms_ref, out_ref, bias_ref):
    err = err_ref[:, :576]
    bias_ref[...] = jnp.sum(err.astype(f32), axis=0, keepdims=True)
    for n in range(4):
        at = slice(n * 256, (n + 1) * 256)
        acts = jnp.concatenate(
            [acts_ref[:, q * 64 : (q + 1) * 64, :].reshape(512, 128) for q in (2 * n, 2 * n + 1)], axis=1
        )
        norms = jnp.concatenate([norms_ref[q : q + 1, :] for q in (2 * n, 2 * n + 1)], axis=1)
        scale = penalty_weight / 16.0 * jnp.sum(acts.astype(f32), axis=0, keepdims=True) / norms
        outer = matmul(err, acts, ((0,), (0,)))
        out_ref[:, at] = (outer + scale * w_ref[:, at].astype(f32)).astype(bf16)


def encoder_gradient(rows_ref, d_pre_ref, out_ref, bias_ref):
    rows = rows_ref[...]
    for n in range(4):
        pair = [d_pre_ref[:, q * 64 : (q + 1) * 64, :].reshape(512, 128) for q in (2 * n, 2 * n + 1)]
        for h in range(2):
            bias_ref[2 * n + h : 2 * n + h + 1, :] = jnp.sum(pair[h].astype(f32), axis=0, keepdims=True)
        d_pre = jnp.concatenate(pair, axis=1)
        out_ref[:, n * 256 : (n + 1) * 256] = matmul(rows, d_pre, ((0,), (0,))).astype(bf16)


def exchange(blocks, axes):
    return lax.all_to_all(blocks, axes, 0, 0, tiled=True)


def block_at(array, at):
    return lax.dynamic_index_in_dim(array, at, 0, keepdims=False)


def split(value):
    high = lax.reduce_precision(value, exponent_bits=8, mantissa_bits=7)
    return high.astype(bf16), (value - high).astype(bf16)


def local(residual, w_enc, b_enc, w_dec, b_dec):
    core, at_x, at_y = lax.axis_index("c"), lax.axis_index("x"), lax.axis_index("yl")
    w_across = w_dec.T
    bias = b_enc.reshape(8, 128)
    work = 2 * 512 * 576 * 1024
    near = exchange(jnp.broadcast_to(residual[None], (32, 8, 576)), CHIPS).reshape(256, 576)
    rows_all = lax.all_gather(near, "c", axis=0, tiled=True)
    wide = w_across.astype(f32)
    squares = jnp.concatenate(split(jnp.sum(wide * wide, axis=0).reshape(8, 128)), axis=0)

    sent, low = call(encode, [((8, 528, 128), bf16), ((8, 512, 128), bf16)], rows_all, w_enc, squares, flops=work)
    acts, pre, norms, penalty = call(
        activate,
        [((8, 512, 128), bf16), ((512, 128), f32), ((8, 128), f32), ((1, 128), f32)],
        exchange(sent, LAYER),
        bias,
    )
    acts = exchange(acts, LAYER)

    half = core.astype(jnp.int32).reshape(1)
    other = call(decode, [((256, 576), bf16)], 1 - half, acts, w_across, flops=work // 2, smem=(0,))[0]
    other = lax.ppermute(other, "c", [(0, 1), (1, 0)])
    mine = call(decode, [((256, 576), f32)], half, acts, w_across, flops=work // 2, smem=(0,))[0]
    pair = (mine + other.astype(f32)).astype(bf16)

    pair, low = lax.optimization_barrier((pair, low))
    low = low.reshape(4, 1024, 128)
    away = at_x ^ 1
    over = jnp.stack([block_at(low, away), block_at(low, 3 - away)])
    over = lax.ppermute(over, "x", [(i, i ^ 1) for i in range(4)])
    recon, over = lax.optimization_barrier((exchange(pair.reshape(32, 8, 576), CHIPS), over))
    own = block_at(low, at_x).astype(f32) + over[0].astype(f32)
    mirror = (block_at(low, 3 - at_x).astype(f32) + over[1].astype(f32)).astype(bf16)

    packed = call(
        residue,
        [((256, 640), bf16)],
        recon.reshape(256, 576),
        b_dec.reshape(1, 576),
        residual.astype(f32),
        penalty,
    )[0]
    packed, mirror = lax.optimization_barrier((packed, mirror))
    mirror = lax.ppermute(mirror, "x", [(i, 3 - i) for i in range(4)])
    packed, mirror = lax.optimization_barrier((exchange(packed.reshape(32, 8, 640), CHIPS), mirror))
    err = lax.all_gather(packed.reshape(256, 640), "c", axis=0, tiled=True)

    sent = call(decode_back, [((8, 528, 128), bf16)], err, w_across, flops=work)[0]
    sent, mirror = lax.optimization_barrier((sent, mirror))
    own = (own + mirror.astype(f32)).reshape(2, 512, 128)
    fine = lax.ppermute(block_at(own, 1 - at_y).astype(bf16), "yl", [(0, 1), (1, 0)])
    fine = block_at(own, at_y) + fine.astype(f32)
    d_pre, loss = call(
        mask, [((8, 512, 128), bf16), ((1, 1), f32)], exchange(sent, LAYER), pre, fine, norms
    )
    grad_dec, grad_bdec = call(
        decoder_gradient, [((576, 1024), bf16), ((1, 576), f32)], acts, err, w_across, norms, flops=work
    )
    grad_enc, grad_benc = call(
        encoder_gradient, [((576, 1024), bf16), ((8, 128), f32)], rows_all, exchange(d_pre, LAYER), flops=work
    )
    return (
        grad_enc,
        grad_benc.astype(bf16).reshape(1024),
        grad_dec.T,
        grad_bdec.astype(bf16).reshape(576),
        loss.reshape(()),
    )


def solution(mesh):
    fine = Mesh(mesh.devices.reshape(4, 2, 8, 4, 2), ("x", "yl", "z", "yh", "c"))
    placed = (P(LATENT, LAYER), P(LAYER, LATENT), P(LATENT), P(LATENT, LAYER), P(LAYER))
    return jax.shard_map(
        local,
        mesh=fine,
        in_specs=placed,
        out_specs=(P(LAYER, LATENT), P(LATENT), P(LATENT, LAYER), P(LAYER), P()),
        check_vma=False,
    )
```

```python
import math

import jax
import jax.numpy as jnp
from jax import lax
from jax.experimental import pallas as pl
from jax.experimental.pallas import tpu as pltpu
from jax.sharding import Mesh, PartitionSpec as P

D = 4608
ROWS = 512
LAYER = ("x", "yl")
TURNS = ("yl", "x")
CHIPS = ("z", "yh")
LATENT = ("z", "yh", "c")
f32, bf16 = jnp.float32, jnp.bfloat16

penalty_weight = 0.5


def call(body, outs, *args, flops=0, smem=(), far=(), far_in=(), scratch=()):
    outs = [pltpu.HBM(*o) if i in far else jax.ShapeDtypeStruct(*o) for i, o in enumerate(outs)]
    size = sum(math.prod(a.shape) * jnp.dtype(a.dtype).itemsize for a in list(args) + outs)

    args = [pltpu.with_memory_space_constraint(a, pltpu.HBM) if i in far_in else a for i, a in enumerate(args)]

    def space(i):
        return pltpu.SMEM if i in smem else pltpu.HBM if i in far_in else pltpu.VMEM

    return pl.pallas_call(
        body,
        out_shape=outs,
        in_specs=[pl.BlockSpec(memory_space=space(i)) for i in range(len(args))],
        out_specs=[pl.BlockSpec(memory_space=pltpu.HBM if i in far else pltpu.VMEM) for i in range(len(outs))],
        scratch_shapes=list(scratch),
        cost_estimate=pl.CostEstimate(flops=flops, bytes_accessed=size, transcendentals=0),
        compiler_params=pltpu.CompilerParams(vmem_limit_bytes=24 * 2**20),
    )(*args)


def copies(source, target, sem, pieces):
    return [pltpu.make_async_copy(source.at[at], target.at[at], sem.at[i]) for i, at in enumerate(pieces)]


def rows_of(lo, hi):
    return (slice(None), pl.ds(lo, hi - lo), slice(None))


def lanes_of(lo, hi):
    return (slice(None), pl.ds(lo, hi - lo))


def matmul(a, b, dims):
    return lax.dot_general(a, b, (dims, ((), ())), preferred_element_type=f32)


def row_block(ref, lo, count):
    parts = [ref[pl.ds(lo, count), q * 64 : (q + 1) * 64, :].reshape(count * 64, 128) for q in range(8)]
    return jnp.concatenate(parts, axis=1)


def spread_rows(rows_ref, out_ref):
    rows = rows_ref[...].astype(f32)
    out_ref[...] = jnp.broadcast_to(rows[None], (32, 8, 576)).reshape(256, 576).astype(bf16)


QUARTERS = [(0, 128), (128, 256), (256, 384), (384, 528)]


def encode(rows_ref, w_ref, squares_ref, sent_ref, low_ref, sent, low, sem, low_sem):
    out = copies(sent, sent_ref, sem, [rows_of(*at) for at in QUARTERS])
    low_out = copies(low, low_ref, low_sem, [rows_of(n * 128, n * 128 + 128) for n in range(4)])
    sent[:, 512:528, :] = jnp.broadcast_to(squares_ref[...][None], (8, 16, 128))
    rows = rows_ref[...]
    for n in range(4):
        part = matmul(rows, w_ref[:, n * 256 : (n + 1) * 256], ((1,), (0,)))
        high = part.astype(bf16)
        rest = (part - high.astype(f32)).astype(bf16)
        for h in range(2):
            at = pl.ds((2 * n + h) * 64, 64)
            sent[:, at, :] = high[:, h * 128 : (h + 1) * 128].reshape(8, 64, 128)
            low[:, at, :] = rest[:, h * 128 : (h + 1) * 128].reshape(8, 64, 128)
        out[n].start()
        low_out[n].start()
    for copy in out + low_out:
        copy.wait()


def arrange(to_ref, low_ref, *out_refs):
    for o, ref in enumerate(out_refs):
        half = pl.ds(256 * (o % 2), 256)
        for y in range(2):
            for slot in range(2):
                ref[y, slot] = low_ref[y * 4 + to_ref[2 * o + slot], half, :]


def add_first(keep_a, keep_b, got_a, got_b, own_ref, pass_a, pass_b):
    for h, (keep, got, over) in enumerate(((keep_a, got_a, pass_a), (keep_b, got_b, pass_b))):
        for y in range(2):
            own_ref[y, 256 * h : 256 * h + 256, :] = keep[y, 0].astype(f32) + got[y, 0].astype(f32)
            over[y] = (keep[y, 1].astype(f32) + got[y, 1].astype(f32)).astype(bf16)


def add_second(y_ref, own_ref, got_a, got_b, keep_ref, pass_ref):
    y = y_ref[0]
    for h, got in enumerate((got_a, got_b)):
        half = slice(256 * h, 256 * h + 256)
        keep_ref[half, :] = own_ref[y, half, :] + got[y].astype(f32)
        pass_ref[half, :] = (own_ref[1 - y, half, :] + got[1 - y].astype(f32)).astype(bf16)


EIGHTHS = [(q * 64, q * 64 + 64) for q in range(8)]


def activate(got_ref, bias_ref, out_ref, pre_out, norms_ref, penalty_ref, acts_ref, pre_ref, sem, pre_sem):
    out = copies(acts_ref, out_ref, sem, [rows_of(*at) for at in EIGHTHS])
    extra = jnp.sum(got_ref[:, 512:528, :].astype(f32), axis=0)
    norms = jnp.sqrt(extra[:8] + extra[8:] + 1e-06)
    norms_ref[...] = norms
    penalty = jnp.zeros((1, 128), f32)
    for q in range(8):
        at = pl.ds(q * 64, 64)
        pre = jnp.sum(got_ref[:, at, :].astype(f32), axis=0) + bias_ref[q : q + 1, :]
        pre_ref[at, :] = pre
        acts = jnp.maximum(pre, 0.0).astype(bf16)
        acts_ref[:, at, :] = jnp.broadcast_to(acts[None], (8, 64, 128))
        out[q].start()
        penalty = penalty + jnp.sum(acts.astype(f32), axis=0, keepdims=True) * norms[q : q + 1, :]
    last = pltpu.make_async_copy(pre_ref, pre_out, pre_sem)
    last.start()
    penalty_ref[...] = penalty_weight * penalty
    last.wait()
    for copy in out:
        copy.wait()


def decode(half_ref, acts_ref, w_ref, out_ref):
    acts = row_block(acts_ref, half_ref[0] * 4, 4)
    out_ref[...] = matmul(acts, w_ref[...], ((1,), (1,))).astype(out_ref.dtype)


def residue(got_ref, bias_ref, residual_ref, penalty_far, out_ref, penalty_ref, sem):
    copy = pltpu.make_async_copy(penalty_far, penalty_ref, sem)
    copy.start()
    recon = jnp.sum(got_ref[...].astype(f32).reshape(32, 8, 576), axis=0) + bias_ref[...]
    err = recon - residual_ref[...]
    copy.wait()
    total = jnp.sum(err * err, axis=(0, 1), keepdims=True) + jnp.sum(penalty_ref[...], axis=(0, 1), keepdims=True)
    high = total.astype(bf16).astype(f32)
    row = lax.broadcasted_iota(jnp.int32, (8, 64), 0)
    lane = lax.broadcasted_iota(jnp.int32, (8, 64), 1)
    tail = jnp.where(row == 0, jnp.where(lane == 0, high, jnp.where(lane == 1, total - high, 0.0)), 0.0)
    block = jnp.concatenate([err / 8.0, tail], axis=1)
    out_ref[...] = jnp.broadcast_to(block[None], (32, 8, 640)).reshape(256, 640).astype(bf16)


def decode_back(err_ref, w_ref, out_ref, sent_ref, sem):
    out = copies(sent_ref, out_ref, sem, [rows_of(*at) for at in QUARTERS])
    err = err_ref[:, :576]
    lane = lax.broadcasted_iota(jnp.int32, (512, 128), 1)
    tail = jnp.where(lane >= 64, err_ref[:, 512:640].astype(f32), 0.0)
    total = jnp.sum(tail, axis=(0, 1), keepdims=True)
    high = total.astype(bf16).astype(f32)
    row = lax.broadcasted_iota(jnp.int32, (16, 128), 0)
    lane = lax.broadcasted_iota(jnp.int32, (16, 128), 1)
    tail = jnp.where(row == 0, jnp.where(lane == 0, high, jnp.where(lane == 1, total - high, 0.0)), 0.0)
    sent_ref[:, 512:528, :] = jnp.broadcast_to(tail.astype(bf16)[None], (8, 16, 128))
    for n in range(4):
        part = matmul(err, w_ref[:, n * 256 : (n + 1) * 256], ((1,), (0,))).astype(bf16)
        for h in range(2):
            at = pl.ds((2 * n + h) * 64, 64)
            sent_ref[:, at, :] = part[:, h * 128 : (h + 1) * 128].reshape(8, 64, 128)
        out[n].start()
    for copy in out:
        copy.wait()


def mask(*refs):
    far_ref, pre_far, fine_far, rest_far, norms_ref, out_ref, loss_ref = refs[:7]
    got_ref, d_pre_ref, pre_ref, fine_ref, rest_ref, in_sem, sem, more_sem = refs[7:]
    more = [
        pltpu.make_async_copy(a, b, more_sem.at[i])
        for i, (a, b) in enumerate(((pre_far, pre_ref), (fine_far, fine_ref), (rest_far, rest_ref)))
    ]
    for copy in more:
        copy.start()
    into = copies(far_ref, got_ref, in_sem, [rows_of(*at) for at in EIGHTHS + [(512, 528)]])
    out = copies(d_pre_ref, out_ref, sem, [rows_of(*at) for at in EIGHTHS])
    for copy in into:
        copy.start()
    for copy in more:
        copy.wait()
    for q in range(8):
        at = pl.ds(q * 64, 64)
        exact = pre_ref[at, :] + (fine_ref[at, :] + rest_ref[at, :].astype(f32))
        into[q].wait()
        d_acts = jnp.sum(got_ref[:, at, :].astype(f32), axis=0)
        d_acts = d_acts + penalty_weight / 16.0 * norms_ref[q : q + 1, :]
        d_pre = jnp.where(exact > 0, d_acts, 0.0).astype(bf16)
        d_pre_ref[:, at, :] = jnp.broadcast_to(d_pre[None], (8, 64, 128))
        out[q].start()
    into[8].wait()
    total = jnp.sum(got_ref[:, 512:528, :].astype(f32), axis=0)
    loss_ref[...] = jnp.sum(total, axis=(0, 1), keepdims=True) / (ROWS * D)
    for copy in out:
        copy.wait()


def decoder_gradient(acts_ref, err_ref, w_ref, norms_ref, out_ref, bias_ref):
    err = err_ref[:, :576]
    bias_ref[...] = jnp.sum(err.astype(f32), axis=0, keepdims=True)
    for n in range(4):
        at = slice(n * 256, (n + 1) * 256)
        acts = jnp.concatenate(
            [acts_ref[:, q * 64 : (q + 1) * 64, :].reshape(512, 128) for q in (2 * n, 2 * n + 1)], axis=1
        )
        norms = jnp.concatenate([norms_ref[q : q + 1, :] for q in (2 * n, 2 * n + 1)], axis=1)
        scale = penalty_weight / 16.0 * jnp.sum(acts.astype(f32), axis=0, keepdims=True) / norms
        outer = matmul(err, acts, ((0,), (0,)))
        out_ref[:, at] = (outer + scale * w_ref[:, at].astype(f32)).astype(bf16)


def turn(rows_ref, out_ref):
    out_ref[...] = rows_ref[...].T


def encoder_gradient(*refs):
    across_far, far_ref, out_ref, bias_ref, across_ref, d_pre_ref, grad_ref, across_sem, in_sem, sem = refs
    first = pltpu.make_async_copy(across_far, across_ref, across_sem)
    first.start()
    into = copies(far_ref, d_pre_ref, in_sem, [rows_of(n * 128, n * 128 + 128) for n in range(4)])
    out = copies(grad_ref, out_ref, sem, [lanes_of(n * 256, n * 256 + 256) for n in range(4)])
    for copy in into:
        copy.start()
    first.wait()
    across = across_ref[...]
    sums = []
    for n in range(4):
        into[n].wait()
        pair = [d_pre_ref[:, q * 64 : (q + 1) * 64, :].reshape(512, 128) for q in (2 * n, 2 * n + 1)]
        d_pre = jnp.concatenate(pair, axis=1)
        grad_ref[:, n * 256 : (n + 1) * 256] = matmul(across, d_pre, ((1,), (0,))).astype(bf16)
        out[n].start()
        sums += [jnp.sum(part.astype(f32), axis=0, keepdims=True) for part in pair]
    bias_ref[...] = jnp.concatenate(sums, axis=0).astype(bf16)
    for copy in out:
        copy.wait()


def exchange(blocks, axes):
    return lax.all_to_all(blocks, axes, 0, 0, tiled=True)


def split(value):
    high = lax.reduce_precision(value, exponent_bits=8, mantissa_bits=7)
    return high.astype(bf16), (value - high).astype(bf16)


def local(residual, w_enc, b_enc, w_dec, b_dec):
    core, at_x, at_y = lax.axis_index("c"), lax.axis_index("x"), lax.axis_index("yl")
    w_across = w_dec.T
    bias = b_enc.reshape(8, 128)
    work = 2 * 512 * 576 * 1024
    block = pltpu.VMEM((8, 528, 128), bf16)
    wide = pltpu.VMEM((8, 512, 128), bf16)
    sems = pltpu.SemaphoreType.DMA
    near = call(spread_rows, [((256, 576), bf16)], residual)[0]
    near = exchange(near.reshape(32, 8, 576), CHIPS).reshape(256, 576)
    rows_all = lax.all_gather(near, "c", axis=0, tiled=True)
    w_wide = w_across.astype(f32)
    squares = jnp.concatenate(split(jnp.sum(w_wide * w_wide, axis=0).reshape(8, 128)), axis=0)

    sent, low = call(
        encode,
        [((8, 528, 128), bf16), ((8, 512, 128), bf16)],
        rows_all,
        w_enc,
        squares,
        flops=work,
        far=(0, 1),
        scratch=(block, wide, sems((4,)), sems((4,))),
    )
    acts, pre, norms, penalty = call(
        activate,
        [((8, 512, 128), bf16), ((512, 128), f32), ((8, 128), f32), ((1, 128), f32)],
        exchange(sent, TURNS),
        bias,
        far=(0, 1),
        scratch=(wide, pltpu.VMEM((512, 128), f32), sems((8,)), sems),
    )
    near_x, far_x = at_x ^ 1, 3 - at_x
    to = jnp.stack([near_x, 3 - near_x, far_x, far_x ^ 1, at_x, far_x, at_x, near_x]).astype(jnp.int32)
    piece = ((2, 2, 256, 128), bf16)
    over_a, over_b, keep_a, keep_b = call(arrange, [piece] * 4, to, low, smem=(0,))
    acts, over_a, over_b = lax.optimization_barrier((exchange(acts, TURNS), over_a, over_b))

    half = core.astype(jnp.int32).reshape(1)
    other = call(decode, [((256, 576), bf16)], 1 - half, acts, w_across, flops=work // 2, smem=(0,))[0]
    other = lax.ppermute(other, "c", [(0, 1), (1, 0)])
    mine = call(decode, [((256, 576), f32)], half, acts, w_across, flops=work // 2, smem=(0,))[0]
    pair = (mine + other.astype(f32)).astype(bf16)

    by_near = [(i, i ^ 1) for i in range(4)]
    by_far = [(i, 3 - i) for i in range(4)]
    pair, over_a, over_b = lax.optimization_barrier((pair, over_a, over_b))
    over_a = lax.ppermute(over_a, "x", by_near)
    over_b = lax.ppermute(over_b, "x", by_far)
    recon, over_a, over_b = lax.optimization_barrier((exchange(pair.reshape(32, 8, 576), CHIPS), over_a, over_b))
    packed = call(
        residue,
        [((256, 640), bf16)],
        recon.reshape(256, 576),
        b_dec.reshape(1, 576),
        residual.astype(f32),
        penalty,
        far_in=(3,),
        scratch=(pltpu.VMEM((1, 128), f32), sems),
    )[0]
    packed, over_a, over_b = lax.optimization_barrier((packed, over_a, over_b))
    part = ((2, 256, 128), bf16)
    own, over_a, over_b = call(add_first, [((2, 512, 128), f32), part, part], keep_a, keep_b, over_a, over_b)
    over_a = lax.ppermute(over_a, "x", by_far)
    over_b = lax.ppermute(over_b, "x", by_near)
    packed = exchange(packed.reshape(32, 8, 640), CHIPS).reshape(256, 640)
    err = lax.all_gather(packed, "c", axis=0, tiled=True)
    err, over_a, over_b = lax.optimization_barrier((err, over_a, over_b))

    sent = call(
        decode_back,
        [((8, 528, 128), bf16)],
        err,
        w_across,
        flops=work,
        far=(0,),
        scratch=(block, sems((4,))),
    )[0]
    sent, over_a, over_b = lax.optimization_barrier((sent, over_a, over_b))
    fine, rest = call(
        add_second,
        [((512, 128), f32), ((512, 128), bf16)],
        at_y.astype(jnp.int32).reshape(1),
        own,
        over_a,
        over_b,
        smem=(0,),
    )
    rest = lax.ppermute(rest, "yl", [(0, 1), (1, 0)])
    d_pre, loss = call(
        mask,
        [((8, 512, 128), bf16), ((1, 1), f32)],
        exchange(sent, TURNS),
        pre,
        fine,
        rest,
        norms,
        far=(0,),
        far_in=(0, 1, 2, 3),
        scratch=(
            block,
            wide,
            pltpu.VMEM((512, 128), f32),
            pltpu.VMEM((512, 128), f32),
            pltpu.VMEM((512, 128), bf16),
            sems((9,)),
            sems((8,)),
            sems((3,)),
        ),
    )
    grad_dec, grad_bdec = call(
        decoder_gradient, [((576, 1024), bf16), ((1, 576), f32)], acts, err, w_across, norms, flops=work
    )
    across = call(turn, [((576, 512), bf16)], rows_all)[0]
    grad_enc, grad_benc = call(
        encoder_gradient,
        [((576, 1024), bf16), ((8, 128), bf16)],
        across,
        exchange(d_pre, TURNS),
        flops=work,
        far=(0,),
        far_in=(0, 1),
        scratch=(
            pltpu.VMEM((576, 512), bf16),
            wide,
            pltpu.VMEM((576, 1024), bf16),
            sems,
            sems((4,)),
            sems((4,)),
        ),
    )
    return (
        grad_enc,
        grad_benc.reshape(1024),
        grad_dec.T,
        grad_bdec.astype(bf16).reshape(576),
        loss.reshape(()),
    )


def solution(mesh):
    fine = Mesh(mesh.devices.reshape(4, 2, 8, 4, 2), ("x", "yl", "z", "yh", "c"))
    placed = (P(LATENT, LAYER), P(LAYER, LATENT), P(LATENT), P(LATENT, LAYER), P(LAYER))
    return jax.shard_map(
        local,
        mesh=fine,
        in_specs=placed,
        out_specs=(P(LAYER, LATENT), P(LATENT), P(LATENT, LAYER), P(LAYER), P()),
        check_vma=False,
    )
```

```python
import jax
import jax.numpy as jnp
from jax import lax
from jax.experimental import pallas as pl
from jax.experimental.pallas import tpu as pltpu
from jax.sharding import Mesh, PartitionSpec as P

D = 4608
ROWS = 512
LAYER = ("x", "yl")
CHIPS = ("z", "yh")
LATENT = ("z", "yh", "c")
f32, bf16 = jnp.float32, jnp.bfloat16

penalty_weight = 0.5


def call(body, outs, *args, flops=0, smem=()):
    outs = [jax.ShapeDtypeStruct(shape, dtype) for shape, dtype in outs]
    size = sum(a.size * a.dtype.itemsize for a in args) + sum(o.size * o.dtype.itemsize for o in outs)
    return pl.pallas_call(
        body,
        out_shape=outs,
        in_specs=[
            pl.BlockSpec(memory_space=pltpu.SMEM if i in smem else pltpu.VMEM) for i in range(len(args))
        ],
        out_specs=[pl.BlockSpec(memory_space=pltpu.VMEM) for _ in outs],
        cost_estimate=pl.CostEstimate(flops=flops, bytes_accessed=size, transcendentals=0),
        compiler_params=pltpu.CompilerParams(vmem_limit_bytes=24 * 2**20),
    )(*args)


def matmul(a, b, dims):
    return lax.dot_general(a, b, (dims, ((), ())), preferred_element_type=f32)


def row_block(ref, lo, count):
    parts = [ref[pl.ds(lo, count), q * 64 : (q + 1) * 64, :].reshape(count * 64, 128) for q in range(8)]
    return jnp.concatenate(parts, axis=1)


STEPS = 252.0


def spread_rows(rows_ref, out_ref):
    rows = rows_ref[...].astype(f32)
    out_ref[...] = jnp.broadcast_to(rows[None], (32, 8, 576)).reshape(256, 576).astype(bf16)


def encode(rows_ref, w_ref, squares_ref, sent_ref):
    rows = rows_ref[...]
    tops = []
    for n in range(4):
        part = matmul(rows, w_ref[:, n * 256 : (n + 1) * 256], ((1,), (0,))).reshape(8, 64, 256)
        size = jnp.abs(part)
        top = (jnp.max(size, axis=1, keepdims=True) * (1 + 2.0**-7) + 1e-30).astype(bf16).astype(f32)
        code = jnp.exp2(size * (STEPS / top) - 126.0)
        code = jnp.where(part < 0, -code, code).astype(bf16)
        for h in range(2):
            at = pl.ds((2 * n + h) * 64, 64)
            lanes = slice(h * 128, (h + 1) * 128)
            sent_ref[:, at, :] = code[:, :, lanes]
            tops.append(top[:, :, lanes])
    squares = jnp.broadcast_to(squares_ref[...][None], (8, 8, 128))
    sent_ref[:, 512:528, :] = jnp.concatenate([squares] + tops, axis=1).astype(bf16)


def activate(got_ref, bias_ref, acts_ref, pre_ref, norms_ref, penalty_ref):
    extra = got_ref[:, 512:528, :].astype(f32)
    norms = jnp.sqrt(jnp.sum(extra[:, :8, :], axis=0) + 1e-06)
    norms_ref[...] = norms
    penalty = jnp.zeros((1, 128), f32)
    for q in range(8):
        at = pl.ds(q * 64, 64)
        code = got_ref[:, at, :].astype(f32)
        part = (jnp.log2(jnp.abs(code)) + 126.0) * (extra[:, 8 + q : 9 + q, :] / STEPS)
        pre = jnp.sum(jnp.where(code < 0, -part, part), axis=0) + bias_ref[q : q + 1, :]
        pre_ref[at, :] = pre
        acts = jnp.maximum(pre, 0.0).astype(bf16)
        acts_ref[:, at, :] = jnp.broadcast_to(acts[None], (8, 64, 128))
        penalty = penalty + jnp.sum(acts.astype(f32), axis=0, keepdims=True) * norms[q : q + 1, :]
    penalty_ref[...] = penalty_weight * penalty


def decode(half_ref, acts_ref, w_ref, out_ref):
    acts = row_block(acts_ref, half_ref[0] * 4, 4)
    out_ref[...] = matmul(acts, w_ref[...], ((1,), (1,))).astype(out_ref.dtype)


def residue(got_ref, bias_ref, residual_ref, penalty_ref, out_ref):
    recon = jnp.sum(got_ref[...].astype(f32).reshape(32, 8, 576), axis=0) + bias_ref[...]
    err = recon - residual_ref[...]
    total = jnp.sum(err * err, axis=(0, 1), keepdims=True) + jnp.sum(penalty_ref[...], axis=(0, 1), keepdims=True)
    high = total.astype(bf16).astype(f32)
    row = lax.broadcasted_iota(jnp.int32, (8, 64), 0)
    lane = lax.broadcasted_iota(jnp.int32, (8, 64), 1)
    tail = jnp.where(row == 0, jnp.where(lane == 0, high, jnp.where(lane == 1, total - high, 0.0)), 0.0)
    block = jnp.concatenate([err / 8.0, tail], axis=1)
    out_ref[...] = jnp.broadcast_to(block[None], (32, 8, 640)).reshape(256, 640).astype(bf16)


def decode_back(err_ref, w_ref, sent_ref):
    err = err_ref[:, :576]
    lane = lax.broadcasted_iota(jnp.int32, (512, 128), 1)
    tail = jnp.where(lane >= 64, err_ref[:, 512:640].astype(f32), 0.0)
    total = jnp.sum(tail, axis=(0, 1), keepdims=True)
    high = total.astype(bf16).astype(f32)
    row = lax.broadcasted_iota(jnp.int32, (16, 128), 0)
    lane = lax.broadcasted_iota(jnp.int32, (16, 128), 1)
    tail = jnp.where(row == 0, jnp.where(lane == 0, high, jnp.where(lane == 1, total - high, 0.0)), 0.0)
    sent_ref[:, 512:528, :] = jnp.broadcast_to(tail.astype(bf16)[None], (8, 16, 128))
    for n in range(4):
        part = matmul(err, w_ref[:, n * 256 : (n + 1) * 256], ((1,), (0,))).astype(bf16)
        for h in range(2):
            at = pl.ds((2 * n + h) * 64, 64)
            sent_ref[:, at, :] = part[:, h * 128 : (h + 1) * 128].reshape(8, 64, 128)


def mask(got_ref, pre_ref, norms_ref, out_ref, loss_ref):
    for q in range(8):
        at = pl.ds(q * 64, 64)
        d_acts = jnp.sum(got_ref[:, at, :].astype(f32), axis=0)
        d_acts = d_acts + penalty_weight / 16.0 * norms_ref[q : q + 1, :]
        d_pre = jnp.where(pre_ref[at, :] > 0, d_acts, 0.0).astype(bf16)
        out_ref[:, at, :] = jnp.broadcast_to(d_pre[None], (8, 64, 128))
    total = jnp.sum(got_ref[:, 512:528, :].astype(f32), axis=0)
    loss_ref[...] = jnp.sum(total, axis=(0, 1), keepdims=True) / (ROWS * D)


def decoder_gradient(acts_ref, err_ref, w_ref, norms_ref, out_ref, bias_ref):
    err = err_ref[:, :576]
    bias_ref[...] = jnp.sum(err.astype(f32), axis=0, keepdims=True).astype(bf16)
    for n in range(4):
        at = slice(n * 256, (n + 1) * 256)
        acts = jnp.concatenate(
            [acts_ref[:, q * 64 : (q + 1) * 64, :].reshape(512, 128) for q in (2 * n, 2 * n + 1)], axis=1
        )
        norms = jnp.concatenate([norms_ref[q : q + 1, :] for q in (2 * n, 2 * n + 1)], axis=1)
        scale = penalty_weight / 16.0 * jnp.sum(acts.astype(f32), axis=0, keepdims=True) / norms
        outer = matmul(err, acts, ((0,), (0,)))
        out_ref[:, at] = (outer + scale * w_ref[:, at].astype(f32)).astype(bf16)


def encoder_gradient(rows_ref, d_pre_ref, out_ref, bias_ref):
    rows = rows_ref[...]
    sums = []
    for n in range(4):
        pair = [d_pre_ref[:, q * 64 : (q + 1) * 64, :].reshape(512, 128) for q in (2 * n, 2 * n + 1)]
        sums += [jnp.sum(part.astype(f32), axis=0, keepdims=True) for part in pair]
        d_pre = jnp.concatenate(pair, axis=1)
        out_ref[:, n * 256 : (n + 1) * 256] = matmul(rows, d_pre, ((0,), (0,))).astype(bf16)
    bias_ref[...] = jnp.concatenate(sums, axis=0).astype(bf16)


def exchange(blocks, axes):
    return lax.all_to_all(blocks, axes, 0, 0, tiled=True)


def local(residual, w_enc, b_enc, w_dec, b_dec):
    w_across = w_dec.T
    work = 2 * 512 * 576 * 1024
    near = call(spread_rows, [((256, 576), bf16)], residual)[0]
    half = lax.axis_index("c").astype(jnp.int32).reshape(1)
    small = (half, 1 - half, b_dec.reshape(1, 576), residual.astype(f32), b_enc.reshape(8, 128))
    near, small = lax.optimization_barrier((exchange(near.reshape(32, 8, 576), CHIPS), small))
    half, other_half, bias_dec, residual, bias_enc = small
    near = near.reshape(256, 576)
    rows_all = lax.all_gather(near, "c", axis=0, tiled=True)
    wide = w_across.astype(f32)
    squares = jnp.sum(wide * wide, axis=0).reshape(8, 128)

    sent = call(encode, [((8, 528, 128), bf16)], rows_all, w_enc, squares, flops=work)[0]
    acts, pre, norms, penalty = call(
        activate,
        [((8, 512, 128), bf16), ((512, 128), f32), ((8, 128), f32), ((1, 128), f32)],
        exchange(sent, LAYER),
        bias_enc,
    )
    acts = exchange(acts, LAYER)

    other = call(decode, [((256, 576), bf16)], other_half, acts, w_across, flops=work // 2, smem=(0,))[0]
    other = lax.ppermute(other, "c", [(0, 1), (1, 0)])
    mine = call(decode, [((256, 576), f32)], half, acts, w_across, flops=work // 2, smem=(0,))[0]
    pair = (mine + other.astype(f32)).astype(bf16)
    recon = exchange(pair.reshape(32, 8, 576), CHIPS)
    packed = call(
        residue,
        [((256, 640), bf16)],
        recon.reshape(256, 576),
        bias_dec,
        residual,
        penalty,
    )[0]
    packed = exchange(packed.reshape(32, 8, 640), CHIPS).reshape(256, 640)
    err = lax.all_gather(packed, "c", axis=0, tiled=True)

    sent = call(decode_back, [((8, 528, 128), bf16)], err, w_across, flops=work)[0]
    got, acts, err = lax.optimization_barrier((exchange(sent, LAYER), acts, err))
    d_pre, loss = call(mask, [((8, 512, 128), bf16), ((1, 1), f32)], got, pre, norms)
    grad_dec, grad_bdec = call(
        decoder_gradient, [((576, 1024), bf16), ((1, 576), bf16)], acts, err, w_across, norms, flops=work
    )
    d_pre, grad_dec, grad_bdec, loss = lax.optimization_barrier(
        (d_pre, grad_dec, grad_bdec.reshape(576), loss.reshape(()))
    )
    grad_enc, grad_benc = call(
        encoder_gradient, [((576, 1024), bf16), ((8, 128), bf16)], rows_all, exchange(d_pre, LAYER), flops=work
    )
    return (
        grad_enc,
        grad_benc.reshape(1024),
        grad_dec.T,
        grad_bdec,
        loss,
    )


def solution(mesh):
    fine = Mesh(mesh.devices.reshape(4, 2, 8, 4, 2), ("x", "yl", "z", "yh", "c"))
    placed = (P(LATENT, LAYER), P(LAYER, LATENT), P(LATENT), P(LATENT, LAYER), P(LAYER))
    return jax.shard_map(
        local,
        mesh=fine,
        in_specs=placed,
        out_specs=(P(LAYER, LATENT), P(LATENT), P(LATENT, LAYER), P(LAYER), P()),
        check_vma=False,
    )
```

```python
import math

import jax
import jax.numpy as jnp
from jax import lax
from jax.experimental import pallas as pl
from jax.experimental.pallas import tpu as pltpu
from jax.sharding import Mesh, PartitionSpec as P

D = 4608
ROWS = 512
LAYER = ("x", "yl")
CHIPS = ("z", "yh")
LATENT = ("z", "yh", "c")
f32, bf16 = jnp.float32, jnp.bfloat16

penalty_weight = 0.5


def call(body, outs, *args, flops=0, smem=(), far=(), scratch=()):
    outs = [pltpu.HBM(*o) if i in far else jax.ShapeDtypeStruct(*o) for i, o in enumerate(outs)]
    size = sum(math.prod(a.shape) * jnp.dtype(a.dtype).itemsize for a in list(args) + outs)
    return pl.pallas_call(
        body,
        out_shape=outs,
        in_specs=[
            pl.BlockSpec(memory_space=pltpu.SMEM if i in smem else pltpu.VMEM) for i in range(len(args))
        ],
        out_specs=[pl.BlockSpec(memory_space=pltpu.HBM if i in far else pltpu.VMEM) for i in range(len(outs))],
        scratch_shapes=list(scratch),
        cost_estimate=pl.CostEstimate(flops=flops, bytes_accessed=size, transcendentals=0),
        compiler_params=pltpu.CompilerParams(vmem_limit_bytes=24 * 2**20),
    )(*args)


def quarters(source, target, sem):
    at = [(slice(None), pl.ds(n * 256, 256)) for n in range(4)]
    return [pltpu.make_async_copy(source.at[i], target.at[i], sem.at[n]) for n, i in enumerate(at)]


def matmul(a, b, dims):
    return lax.dot_general(a, b, (dims, ((), ())), preferred_element_type=f32)


def row_block(ref, lo, count):
    parts = [ref[pl.ds(lo, count), q * 64 : (q + 1) * 64, :].reshape(count * 64, 128) for q in range(8)]
    return jnp.concatenate(parts, axis=1)


STEPS = 252.0


def spread_rows(rows_ref, out_ref):
    rows = rows_ref[...].astype(f32)
    out_ref[...] = jnp.broadcast_to(rows[None], (32, 8, 576)).reshape(256, 576).astype(bf16)


def encode(rows_ref, w_ref, squares_ref, sent_ref):
    rows = rows_ref[...]
    tops = []
    for n in range(4):
        part = matmul(rows, w_ref[:, n * 256 : (n + 1) * 256], ((1,), (0,))).reshape(8, 64, 256)
        size = jnp.abs(part)
        top = (jnp.max(size, axis=1, keepdims=True) * (1 + 2.0**-7) + 1e-30).astype(bf16).astype(f32)
        code = jnp.exp2(size * (STEPS / top) - 126.0)
        code = jnp.where(part < 0, -code, code).astype(bf16)
        for h in range(2):
            at = pl.ds((2 * n + h) * 64, 64)
            lanes = slice(h * 128, (h + 1) * 128)
            sent_ref[:, at, :] = code[:, :, lanes]
            tops.append(top[:, :, lanes])
    squares = jnp.broadcast_to(squares_ref[...][None], (8, 8, 128))
    sent_ref[:, 512:528, :] = jnp.concatenate([squares] + tops, axis=1).astype(bf16)


def activate(got_ref, bias_ref, acts_ref, pre_ref, norms_ref, penalty_ref):
    extra = got_ref[:, 512:528, :].astype(f32)
    norms = jnp.sqrt(jnp.sum(extra[:, :8, :], axis=0) + 1e-06)
    norms_ref[...] = norms
    penalty = jnp.zeros((1, 128), f32)
    for q in range(8):
        at = pl.ds(q * 64, 64)
        code = got_ref[:, at, :].astype(f32)
        part = (jnp.log2(jnp.abs(code)) + 126.0) * (extra[:, 8 + q : 9 + q, :] / STEPS)
        pre = jnp.sum(jnp.where(code < 0, -part, part), axis=0) + bias_ref[q : q + 1, :]
        pre_ref[at, :] = pre
        acts = jnp.maximum(pre, 0.0).astype(bf16)
        acts_ref[:, at, :] = jnp.broadcast_to(acts[None], (8, 64, 128))
        penalty = penalty + jnp.sum(acts.astype(f32), axis=0, keepdims=True) * norms[q : q + 1, :]
    penalty_ref[...] = penalty_weight * penalty


def decode(half_ref, acts_ref, w_ref, other_ref, mine_ref):
    for half, ref in ((1 - half_ref[0], other_ref), (half_ref[0], mine_ref)):
        acts = row_block(acts_ref, half * 4, 4)
        ref[...] = matmul(acts, w_ref[...], ((1,), (1,))).astype(ref.dtype)


def add_pair(half_ref, both_ref, mine_ref, out_ref):
    other = both_ref[pl.ds(pl.multiple_of((1 - half_ref[0]) * 256, 256), 256), :]
    out_ref[...] = (mine_ref[...] + other.astype(f32)).astype(bf16)


def residue(got_ref, bias_ref, residual_ref, penalty_ref, out_ref):
    recon = jnp.sum(got_ref[...].astype(f32).reshape(32, 8, 576), axis=0) + bias_ref[...]
    err = recon - residual_ref[...]
    total = jnp.sum(err * err, axis=(0, 1), keepdims=True) + jnp.sum(penalty_ref[...], axis=(0, 1), keepdims=True)
    high = total.astype(bf16).astype(f32)
    row = lax.broadcasted_iota(jnp.int32, (8, 64), 0)
    lane = lax.broadcasted_iota(jnp.int32, (8, 64), 1)
    tail = jnp.where(row == 0, jnp.where(lane == 0, high, jnp.where(lane == 1, total - high, 0.0)), 0.0)
    block = jnp.concatenate([err / 8.0, tail], axis=1)
    out_ref[...] = jnp.broadcast_to(block[None], (32, 8, 640)).reshape(256, 640).astype(bf16)


def decode_back(err_ref, w_ref, sent_ref):
    err = err_ref[:, :576]
    lane = lax.broadcasted_iota(jnp.int32, (512, 128), 1)
    tail = jnp.where(lane >= 64, err_ref[:, 512:640].astype(f32), 0.0)
    total = jnp.sum(tail, axis=(0, 1), keepdims=True)
    high = total.astype(bf16).astype(f32)
    row = lax.broadcasted_iota(jnp.int32, (16, 128), 0)
    lane = lax.broadcasted_iota(jnp.int32, (16, 128), 1)
    tail = jnp.where(row == 0, jnp.where(lane == 0, high, jnp.where(lane == 1, total - high, 0.0)), 0.0)
    sent_ref[:, 512:528, :] = jnp.broadcast_to(tail.astype(bf16)[None], (8, 16, 128))
    for n in range(4):
        part = matmul(err, w_ref[:, n * 256 : (n + 1) * 256], ((1,), (0,))).astype(bf16)
        for h in range(2):
            at = pl.ds((2 * n + h) * 64, 64)
            sent_ref[:, at, :] = part[:, h * 128 : (h + 1) * 128].reshape(8, 64, 128)


def mask(got_ref, pre_ref, norms_ref, out_ref, loss_ref):
    for q in range(8):
        at = pl.ds(q * 64, 64)
        d_acts = jnp.sum(got_ref[:, at, :].astype(f32), axis=0)
        d_acts = d_acts + penalty_weight / 16.0 * norms_ref[q : q + 1, :]
        d_pre = jnp.where(pre_ref[at, :] > 0, d_acts, 0.0).astype(bf16)
        out_ref[:, at, :] = jnp.broadcast_to(d_pre[None], (8, 64, 128))
    total = jnp.sum(got_ref[:, 512:528, :].astype(f32), axis=0)
    loss_ref[...] = jnp.sum(total, axis=(0, 1), keepdims=True) / (ROWS * D)


def decoder_gradient(acts_ref, err_ref, w_ref, norms_ref, far_ref, bias_ref, out_ref, sem):
    out = quarters(out_ref, far_ref, sem)
    err = err_ref[:, :576]
    bias_ref[...] = jnp.sum(err.astype(f32), axis=0).astype(bf16)
    for n in range(4):
        at = slice(n * 256, (n + 1) * 256)
        acts = jnp.concatenate(
            [acts_ref[:, q * 64 : (q + 1) * 64, :].reshape(512, 128) for q in (2 * n, 2 * n + 1)], axis=1
        )
        norms = jnp.concatenate([norms_ref[q : q + 1, :] for q in (2 * n, 2 * n + 1)], axis=1)
        scale = penalty_weight / 16.0 * jnp.sum(acts.astype(f32), axis=0, keepdims=True) / norms
        outer = matmul(err, acts, ((0,), (0,)))
        out_ref[:, at] = (outer + scale * w_ref[:, at].astype(f32)).astype(bf16)
        out[n].start()
    for copy in out:
        copy.wait()


def encoder_gradient(rows_ref, d_pre_ref, far_ref, bias_ref, out_ref, sem):
    out = quarters(out_ref, far_ref, sem)
    rows = rows_ref[...]
    sums = []
    for n in range(4):
        pair = [d_pre_ref[:, q * 64 : (q + 1) * 64, :].reshape(512, 128) for q in (2 * n, 2 * n + 1)]
        sums += [jnp.sum(part.astype(f32), axis=0, keepdims=True) for part in pair]
        d_pre = jnp.concatenate(pair, axis=1)
        out_ref[:, n * 256 : (n + 1) * 256] = matmul(rows, d_pre, ((0,), (0,))).astype(bf16)
        out[n].start()
    bias_ref[...] = jnp.concatenate(sums, axis=0).astype(bf16)
    for copy in out:
        copy.wait()


def exchange(blocks, axes):
    return lax.all_to_all(blocks, axes, 0, 0, tiled=True)


def local(residual, w_enc, b_enc, w_dec, b_dec):
    w_across = w_dec.T
    work = 2 * 512 * 576 * 1024
    near = call(spread_rows, [((256, 576), bf16)], residual)[0]
    half = lax.axis_index("c").astype(jnp.int32).reshape(1)
    small = (half, b_dec.reshape(1, 576), residual.astype(f32), b_enc.reshape(8, 128))
    near, small = lax.optimization_barrier((exchange(near.reshape(32, 8, 576), CHIPS), small))
    half, bias_dec, residual, bias_enc = small
    near = near.reshape(256, 576)
    rows_all = lax.all_gather(near, "c", axis=0, tiled=True)
    wide = w_across.astype(f32)
    squares = jnp.sum(wide * wide, axis=0).reshape(8, 128)

    sent = call(encode, [((8, 528, 128), bf16)], rows_all, w_enc, squares, flops=work)[0]
    acts, pre, norms, penalty = call(
        activate,
        [((8, 512, 128), bf16), ((512, 128), f32), ((8, 128), f32), ((1, 128), f32)],
        exchange(sent, LAYER),
        bias_enc,
    )
    acts = exchange(acts, LAYER)

    other, mine = call(
        decode, [((256, 576), bf16), ((256, 576), f32)], half, acts, w_across, flops=work, smem=(0,)
    )
    both = lax.all_gather(other, "c", axis=0, tiled=True)
    pair = call(add_pair, [((256, 576), bf16)], half, both, mine, smem=(0,))[0]
    recon = exchange(pair.reshape(32, 8, 576), CHIPS)
    packed = call(
        residue,
        [((256, 640), bf16)],
        recon.reshape(256, 576),
        bias_dec,
        residual,
        penalty,
    )[0]
    packed = exchange(packed.reshape(32, 8, 640), CHIPS).reshape(256, 640)
    err = lax.all_gather(packed, "c", axis=0, tiled=True)

    sent = call(decode_back, [((8, 528, 128), bf16)], err, w_across, flops=work)[0]
    got, acts, err = lax.optimization_barrier((exchange(sent, LAYER), acts, err))
    d_pre, loss = call(mask, [((8, 512, 128), bf16), ((1, 1), f32)], got, pre, norms)
    kept = dict(flops=work, far=(0,), scratch=(pltpu.VMEM((576, 1024), bf16), pltpu.SemaphoreType.DMA((4,))))
    grad_dec, grad_bdec = call(
        decoder_gradient, [((576, 1024), bf16), ((576,), bf16)], acts, err, w_across, norms, **kept
    )
    d_pre, grad_dec, grad_bdec, loss = lax.optimization_barrier(
        (d_pre, grad_dec, grad_bdec.reshape(576), loss.reshape(()))
    )
    grad_enc, grad_benc = call(
        encoder_gradient, [((576, 1024), bf16), ((8, 128), bf16)], rows_all, exchange(d_pre, LAYER), **kept
    )
    return (
        grad_enc,
        grad_benc.reshape(1024),
        grad_dec.T,
        grad_bdec,
        loss,
    )


def solution(mesh):
    fine = Mesh(mesh.devices.reshape(4, 2, 8, 4, 2), ("x", "yl", "z", "yh", "c"))
    placed = (P(LATENT, LAYER), P(LAYER, LATENT), P(LATENT), P(LATENT, LAYER), P(LAYER))
    return jax.shard_map(
        local,
        mesh=fine,
        in_specs=placed,
        out_specs=(P(LAYER, LATENT), P(LATENT), P(LATENT, LAYER), P(LAYER), P()),
        check_vma=False,
    )
```

```python
import math

import jax
import jax.numpy as jnp
from jax import lax
from jax.experimental import pallas as pl
from jax.experimental.pallas import tpu as pltpu
from jax.sharding import Mesh, PartitionSpec as P

D = 4608
ROWS = 512
LAYER = ("x", "yl")
CHIPS = ("z", "yh")
LATENT = ("z", "yh", "c")
f32, bf16 = jnp.float32, jnp.bfloat16

penalty_weight = 0.5


def call(body, outs, *args, flops=0, smem=(), far=(), scratch=()):
    outs = [jax.ShapeDtypeStruct(*o) for o in outs]
    size = sum(math.prod(a.shape) * jnp.dtype(a.dtype).itemsize for a in list(args) + outs)
    args = [pltpu.with_memory_space_constraint(a, pltpu.HBM) if i in far else a for i, a in enumerate(args)]

    def space(i):
        return pltpu.SMEM if i in smem else pltpu.HBM if i in far else pltpu.VMEM

    return pl.pallas_call(
        body,
        out_shape=outs,
        in_specs=[pl.BlockSpec(memory_space=space(i)) for i in range(len(args))],
        out_specs=[pl.BlockSpec(memory_space=pltpu.VMEM) for _ in outs],
        scratch_shapes=list(scratch),
        cost_estimate=pl.CostEstimate(flops=flops, bytes_accessed=size, transcendentals=0),
        compiler_params=pltpu.CompilerParams(vmem_limit_bytes=24 * 2**20),
    )(*args)


def matmul(a, b, dims):
    return lax.dot_general(a, b, (dims, ((), ())), preferred_element_type=f32)


def row_block(ref, lo, count):
    parts = [ref[pl.ds(lo, count), q * 64 : (q + 1) * 64, :].reshape(count * 64, 128) for q in range(8)]
    return jnp.concatenate(parts, axis=1)


STEPS = 252.0


def spread_rows(rows_ref, out_ref):
    rows = rows_ref[...].astype(f32)
    out_ref[...] = jnp.broadcast_to(rows[None], (32, 8, 576)).reshape(256, 576).astype(bf16)


def encode(rows_ref, w_far, across_ref, sent_ref, w_ref, sem):
    quarters = [(slice(None), pl.ds(n * 256, 256)) for n in range(4)]
    fetch = [pltpu.make_async_copy(w_far.at[at], w_ref.at[at], sem.at[n]) for n, at in enumerate(quarters)]
    for copy in fetch:
        copy.start()
    squares = []
    for q in range(8):
        wide = across_ref[:, q * 128 : (q + 1) * 128].astype(f32)
        squares.append(jnp.sum(wide * wide, axis=0, keepdims=True))
    rows = rows_ref[...]
    tops = []
    for n in range(4):
        fetch[n].wait()
        part = matmul(rows, w_ref[:, n * 256 : (n + 1) * 256], ((1,), (0,))).reshape(8, 64, 256)
        size = jnp.abs(part)
        top = (jnp.max(size, axis=1, keepdims=True) * (1 + 2.0**-7) + 1e-30).astype(bf16).astype(f32)
        code = jnp.exp2(size * (STEPS / top) - 126.0)
        code = jnp.where(part < 0, -code, code).astype(bf16)
        for h in range(2):
            at = pl.ds((2 * n + h) * 64, 64)
            lanes = slice(h * 128, (h + 1) * 128)
            sent_ref[:, at, :] = code[:, :, lanes]
            tops.append(top[:, :, lanes])
    squares = jnp.broadcast_to(jnp.concatenate(squares, axis=0)[None], (8, 8, 128))
    sent_ref[:, 512:528, :] = jnp.concatenate([squares] + tops, axis=1).astype(bf16)


def activate(got_ref, bias_ref, acts_ref, pre_ref, norms_ref, penalty_ref):
    extra = got_ref[:, 512:528, :].astype(f32)
    norms = jnp.sqrt(jnp.sum(extra[:, :8, :], axis=0) + 1e-06)
    norms_ref[...] = norms
    penalty = jnp.zeros((1, 128), f32)
    for q in range(8):
        at = pl.ds(q * 64, 64)
        code = got_ref[:, at, :].astype(f32)
        part = (jnp.log2(jnp.abs(code)) + 126.0) * (extra[:, 8 + q : 9 + q, :] / STEPS)
        pre = jnp.sum(jnp.where(code < 0, -part, part), axis=0) + bias_ref[q : q + 1, :]
        pre_ref[at, :] = pre
        acts = jnp.maximum(pre, 0.0).astype(bf16)
        acts_ref[:, at, :] = jnp.broadcast_to(acts[None], (8, 64, 128))
        penalty = penalty + jnp.sum(acts.astype(f32), axis=0, keepdims=True) * norms[q : q + 1, :]
    penalty_ref[...] = penalty_weight * penalty


def decode(half_ref, acts_ref, w_ref, other_ref, mine_ref):
    for half, ref in ((1 - half_ref[0], other_ref), (half_ref[0], mine_ref)):
        acts = row_block(acts_ref, half * 4, 4)
        ref[...] = matmul(acts, w_ref[...], ((1,), (1,))).astype(ref.dtype)


def add_pair(half_ref, both_ref, mine_ref, out_ref):
    other = both_ref[pl.ds(pl.multiple_of((1 - half_ref[0]) * 256, 256), 256), :]
    out_ref[...] = (mine_ref[...] + other.astype(f32)).astype(bf16)


def residue(got_ref, bias_ref, residual_ref, penalty_ref, out_ref):
    recon = jnp.sum(got_ref[...].astype(f32).reshape(32, 8, 576), axis=0) + bias_ref[...][None, :]
    err = recon - residual_ref[...].astype(f32)
    total = jnp.sum(err * err, axis=(0, 1), keepdims=True) + jnp.sum(penalty_ref[...], axis=(0, 1), keepdims=True)
    high = total.astype(bf16).astype(f32)
    row = lax.broadcasted_iota(jnp.int32, (8, 64), 0)
    lane = lax.broadcasted_iota(jnp.int32, (8, 64), 1)
    tail = jnp.where(row == 0, jnp.where(lane == 0, high, jnp.where(lane == 1, total - high, 0.0)), 0.0)
    block = jnp.concatenate([err / 8.0, tail], axis=1)
    out_ref[...] = jnp.broadcast_to(block[None], (32, 8, 640)).reshape(256, 640).astype(bf16)


def decode_back(err_ref, w_ref, sent_ref):
    err = err_ref[:, :576]
    lane = lax.broadcasted_iota(jnp.int32, (512, 128), 1)
    tail = jnp.where(lane >= 64, err_ref[:, 512:640].astype(f32), 0.0)
    total = jnp.sum(tail, axis=(0, 1), keepdims=True)
    high = total.astype(bf16).astype(f32)
    row = lax.broadcasted_iota(jnp.int32, (16, 128), 0)
    lane = lax.broadcasted_iota(jnp.int32, (16, 128), 1)
    tail = jnp.where(row == 0, jnp.where(lane == 0, high, jnp.where(lane == 1, total - high, 0.0)), 0.0)
    sent_ref[:, 512:528, :] = jnp.broadcast_to(tail.astype(bf16)[None], (8, 16, 128))
    for n in range(4):
        part = matmul(err, w_ref[:, n * 256 : (n + 1) * 256], ((1,), (0,))).astype(bf16)
        for h in range(2):
            at = pl.ds((2 * n + h) * 64, 64)
            sent_ref[:, at, :] = part[:, h * 128 : (h + 1) * 128].reshape(8, 64, 128)


def mask(got_ref, pre_ref, norms_ref, out_ref, loss_ref):
    for q in range(8):
        at = pl.ds(q * 64, 64)
        d_acts = jnp.sum(got_ref[:, at, :].astype(f32), axis=0)
        d_acts = d_acts + penalty_weight / 16.0 * norms_ref[q : q + 1, :]
        d_pre = jnp.where(pre_ref[at, :] > 0, d_acts, 0.0).astype(bf16)
        out_ref[:, at, :] = jnp.broadcast_to(d_pre[None], (8, 64, 128))
    total = jnp.sum(got_ref[:, 512:528, :].astype(f32), axis=0)
    loss_ref[...] = jnp.sum(total, axis=(0, 1), keepdims=True) / (ROWS * D)


def decoder_gradient(acts_ref, err_ref, w_ref, norms_ref, out_ref, bias_ref):
    err = err_ref[:, :576]
    bias_ref[...] = jnp.sum(err.astype(f32), axis=0).astype(bf16)
    for n in range(4):
        at = slice(n * 256, (n + 1) * 256)
        acts = jnp.concatenate(
            [acts_ref[:, q * 64 : (q + 1) * 64, :].reshape(512, 128) for q in (2 * n, 2 * n + 1)], axis=1
        )
        norms = jnp.concatenate([norms_ref[q : q + 1, :] for q in (2 * n, 2 * n + 1)], axis=1)
        scale = penalty_weight / 16.0 * jnp.sum(acts.astype(f32), axis=0, keepdims=True) / norms
        outer = matmul(err, acts, ((0,), (0,)))
        out_ref[:, at] = (outer + scale * w_ref[:, at].astype(f32)).astype(bf16)


def encoder_gradient(rows_ref, d_pre_ref, out_ref, bias_ref):
    rows = rows_ref[...]
    sums = []
    for n in range(4):
        pair = [d_pre_ref[:, q * 64 : (q + 1) * 64, :].reshape(512, 128) for q in (2 * n, 2 * n + 1)]
        sums += [jnp.sum(part.astype(f32), axis=0, keepdims=True) for part in pair]
        d_pre = jnp.concatenate(pair, axis=1)
        out_ref[:, n * 256 : (n + 1) * 256] = matmul(rows, d_pre, ((0,), (0,))).astype(bf16)
    bias_ref[...] = jnp.concatenate(sums, axis=0).astype(bf16)


def exchange(blocks, axes):
    return lax.all_to_all(blocks, axes, 0, 0, tiled=True)


def local(residual, w_enc, b_enc, w_dec, b_dec):
    w_across = w_dec.T
    work = 2 * 512 * 576 * 1024
    near = call(spread_rows, [((256, 576), bf16)], residual)[0]
    half = lax.axis_index("c").astype(jnp.int32).reshape(1)
    near, half = lax.optimization_barrier((near, half))
    near = exchange(near.reshape(32, 8, 576), CHIPS).reshape(256, 576)
    rows_all = lax.all_gather(near, "c", axis=0, tiled=True)
    sent = call(
        encode,
        [((8, 528, 128), bf16)],
        rows_all,
        w_enc,
        w_across,
        flops=work,
        far=(1,),
        scratch=(pltpu.VMEM((576, 1024), bf16), pltpu.SemaphoreType.DMA((4,))),
    )[0]
    acts, pre, norms, penalty = call(
        activate,
        [((8, 512, 128), bf16), ((512, 128), f32), ((8, 128), f32), ((1, 128), f32)],
        exchange(sent, LAYER),
        b_enc.reshape(8, 128),
    )
    acts = exchange(acts, LAYER)

    other, mine = call(
        decode, [((256, 576), bf16), ((256, 576), f32)], half, acts, w_across, flops=work, smem=(0,)
    )
    both = lax.all_gather(other, "c", axis=0, tiled=True)
    pair = call(add_pair, [((256, 576), bf16)], half, both, mine, smem=(0,))[0]
    recon = exchange(pair.reshape(32, 8, 576), CHIPS)
    packed = call(
        residue,
        [((256, 640), bf16)],
        recon.reshape(256, 576),
        b_dec,
        residual,
        penalty,
    )[0]
    packed = exchange(packed.reshape(32, 8, 640), CHIPS).reshape(256, 640)
    err = lax.all_gather(packed, "c", axis=0, tiled=True)

    sent = call(decode_back, [((8, 528, 128), bf16)], err, w_across, flops=work)[0]
    got, acts, err = lax.optimization_barrier((exchange(sent, LAYER), acts, err))
    d_pre, loss = call(mask, [((8, 512, 128), bf16), ((1, 1), f32)], got, pre, norms)
    grad_dec, grad_bdec = call(
        decoder_gradient, [((576, 1024), bf16), ((576,), bf16)], acts, err, w_across, norms, flops=work
    )
    d_pre, grad_dec, grad_bdec, loss = lax.optimization_barrier(
        (d_pre, grad_dec, grad_bdec.reshape(576), loss.reshape(()))
    )
    grad_enc, grad_benc = call(
        encoder_gradient, [((576, 1024), bf16), ((8, 128), bf16)], rows_all, exchange(d_pre, LAYER), flops=work
    )
    return (
        grad_enc,
        grad_benc.reshape(1024),
        grad_dec.T,
        grad_bdec,
        loss,
    )


def solution(mesh):
    fine = Mesh(mesh.devices.reshape(4, 2, 8, 4, 2), ("x", "yl", "z", "yh", "c"))
    placed = (P(LATENT, LAYER), P(LAYER, LATENT), P(LATENT), P(LATENT, LAYER), P(LAYER))
    return jax.shard_map(
        local,
        mesh=fine,
        in_specs=placed,
        out_specs=(P(LAYER, LATENT), P(LATENT), P(LATENT, LAYER), P(LAYER), P()),
        check_vma=False,
    )
```

```python
import math

import jax
import jax.numpy as jnp
from jax import lax
from jax.experimental import pallas as pl
from jax.experimental.pallas import tpu as pltpu
from jax.sharding import Mesh, PartitionSpec as P

D = 4608
ROWS = 512
LAYER = ("x", "yl")
CHIPS = ("z", "yh")
LATENT = ("z", "yh", "c")
f32, bf16 = jnp.float32, jnp.bfloat16

penalty_weight = 0.5


def call(body, outs, *args, flops=0, smem=(), far=(), scratch=()):
    outs = [pltpu.HBM(*o) if i in far else jax.ShapeDtypeStruct(*o) for i, o in enumerate(outs)]
    size = sum(math.prod(a.shape) * jnp.dtype(a.dtype).itemsize for a in list(args) + outs)
    return pl.pallas_call(
        body,
        out_shape=outs,
        in_specs=[
            pl.BlockSpec(memory_space=pltpu.SMEM if i in smem else pltpu.VMEM) for i in range(len(args))
        ],
        out_specs=[pl.BlockSpec(memory_space=pltpu.HBM if i in far else pltpu.VMEM) for i in range(len(outs))],
        scratch_shapes=list(scratch),
        cost_estimate=pl.CostEstimate(flops=flops, bytes_accessed=size, transcendentals=0),
        compiler_params=pltpu.CompilerParams(vmem_limit_bytes=24 * 2**20),
    )(*args)


def matmul(a, b, dims):
    return lax.dot_general(a, b, (dims, ((), ())), preferred_element_type=f32)


def row_block(ref, lo, count):
    parts = [ref[pl.ds(lo, count), q * 64 : (q + 1) * 64, :].reshape(count * 64, 128) for q in range(8)]
    return jnp.concatenate(parts, axis=1)


STEPS = 252.0


def spread_rows(rows_ref, across_ref, out_ref, squares_ref):
    rows = rows_ref[...].astype(f32)
    out_ref[...] = jnp.broadcast_to(rows[None], (32, 8, 576)).reshape(256, 576).astype(bf16)
    for q in range(8):
        wide = across_ref[:, q * 128 : (q + 1) * 128].astype(f32)
        squares_ref[q : q + 1, :] = jnp.sum(wide * wide, axis=0, keepdims=True)


def encode(rows_ref, w_ref, squares_ref, sent_ref):
    rows = rows_ref[...]
    tops = []
    for n in range(4):
        part = matmul(rows, w_ref[:, n * 256 : (n + 1) * 256], ((1,), (0,))).reshape(8, 64, 256)
        size = jnp.abs(part)
        top = (jnp.max(size, axis=1, keepdims=True) * (1 + 2.0**-7) + 1e-30).astype(bf16).astype(f32)
        code = jnp.exp2(size * (STEPS / top) - 126.0)
        code = jnp.where(part < 0, -code, code).astype(bf16)
        for h in range(2):
            at = pl.ds((2 * n + h) * 64, 64)
            lanes = slice(h * 128, (h + 1) * 128)
            sent_ref[:, at, :] = code[:, :, lanes]
            tops.append(top[:, :, lanes])
    squares = jnp.broadcast_to(squares_ref[...][None], (8, 8, 128))
    sent_ref[:, 512:528, :] = jnp.concatenate([squares] + tops, axis=1).astype(bf16)


def activate(got_ref, bias_ref, acts_ref, pre_ref, norms_ref, penalty_ref):
    extra = got_ref[:, 512:528, :].astype(f32)
    norms = jnp.sqrt(jnp.sum(extra[:, :8, :], axis=0) + 1e-06)
    norms_ref[...] = norms
    penalty = jnp.zeros((1, 128), f32)
    for q in range(8):
        at = pl.ds(q * 64, 64)
        code = got_ref[:, at, :].astype(f32)
        part = (jnp.log2(jnp.abs(code)) + 126.0) * (extra[:, 8 + q : 9 + q, :] / STEPS)
        pre = jnp.sum(jnp.where(code < 0, -part, part), axis=0) + bias_ref[q : q + 1, :]
        pre_ref[at, :] = pre
        acts = jnp.maximum(pre, 0.0).astype(bf16)
        acts_ref[:, at, :] = jnp.broadcast_to(acts[None], (8, 64, 128))
        penalty = penalty + jnp.sum(acts.astype(f32), axis=0, keepdims=True) * norms[q : q + 1, :]
    penalty_ref[...] = penalty_weight * penalty


def decode(half_ref, acts_ref, w_ref, other_ref, mine_ref):
    for half, ref in ((1 - half_ref[0], other_ref), (half_ref[0], mine_ref)):
        acts = row_block(acts_ref, half * 4, 4)
        ref[...] = matmul(acts, w_ref[...], ((1,), (1,))).astype(ref.dtype)


def add_pair(half_ref, both_ref, mine_ref, out_ref):
    other = both_ref[pl.ds(pl.multiple_of((1 - half_ref[0]) * 256, 256), 256), :]
    out_ref[...] = (mine_ref[...] + other.astype(f32)).astype(bf16)


def residue(got_ref, bias_ref, residual_ref, penalty_ref, out_ref):
    recon = jnp.sum(got_ref[...].astype(f32).reshape(32, 8, 576), axis=0) + bias_ref[...][None, :]
    err = recon - residual_ref[...].astype(f32)
    total = jnp.sum(err * err, axis=(0, 1), keepdims=True) + jnp.sum(penalty_ref[...], axis=(0, 1), keepdims=True)
    high = total.astype(bf16).astype(f32)
    row = lax.broadcasted_iota(jnp.int32, (8, 64), 0)
    lane = lax.broadcasted_iota(jnp.int32, (8, 64), 1)
    tail = jnp.where(row == 0, jnp.where(lane == 0, high, jnp.where(lane == 1, total - high, 0.0)), 0.0)
    block = jnp.concatenate([err / 8.0, tail], axis=1)
    out_ref[...] = jnp.broadcast_to(block[None], (32, 8, 640)).reshape(256, 640).astype(bf16)


def decode_back(err_ref, w_ref, sent_ref):
    err = err_ref[:, :576]
    lane = lax.broadcasted_iota(jnp.int32, (512, 128), 1)
    tail = jnp.where(lane >= 64, err_ref[:, 512:640].astype(f32), 0.0)
    total = jnp.sum(tail, axis=(0, 1), keepdims=True)
    high = total.astype(bf16).astype(f32)
    row = lax.broadcasted_iota(jnp.int32, (16, 128), 0)
    lane = lax.broadcasted_iota(jnp.int32, (16, 128), 1)
    tail = jnp.where(row == 0, jnp.where(lane == 0, high, jnp.where(lane == 1, total - high, 0.0)), 0.0)
    sent_ref[:, 512:528, :] = jnp.broadcast_to(tail.astype(bf16)[None], (8, 16, 128))
    for n in range(4):
        part = matmul(err, w_ref[:, n * 256 : (n + 1) * 256], ((1,), (0,))).astype(bf16)
        for h in range(2):
            at = pl.ds((2 * n + h) * 64, 64)
            sent_ref[:, at, :] = part[:, h * 128 : (h + 1) * 128].reshape(8, 64, 128)


def mask(got_ref, pre_ref, norms_ref, out_ref, loss_ref):
    for q in range(8):
        at = pl.ds(q * 64, 64)
        d_acts = jnp.sum(got_ref[:, at, :].astype(f32), axis=0)
        d_acts = d_acts + penalty_weight / 16.0 * norms_ref[q : q + 1, :]
        d_pre = jnp.where(pre_ref[at, :] > 0, d_acts, 0.0).astype(bf16)
        out_ref[:, at, :] = jnp.broadcast_to(d_pre[None], (8, 64, 128))
    total = jnp.sum(got_ref[:, 512:528, :].astype(f32), axis=0)
    loss_ref[...] = jnp.sum(total, axis=(0, 1), keepdims=True) / (ROWS * D)


def decoder_gradient(acts_ref, err_ref, w_ref, norms_ref, out_ref, bias_ref):
    err = err_ref[:, :576]
    bias_ref[...] = jnp.sum(err.astype(f32), axis=0).astype(bf16)
    for n in range(4):
        at = slice(n * 256, (n + 1) * 256)
        acts = jnp.concatenate(
            [acts_ref[:, q * 64 : (q + 1) * 64, :].reshape(512, 128) for q in (2 * n, 2 * n + 1)], axis=1
        )
        norms = jnp.concatenate([norms_ref[q : q + 1, :] for q in (2 * n, 2 * n + 1)], axis=1)
        scale = penalty_weight / 16.0 * jnp.sum(acts.astype(f32), axis=0, keepdims=True) / norms
        outer = matmul(err, acts, ((0,), (0,)))
        out_ref[:, at] = (outer + scale * w_ref[:, at].astype(f32)).astype(bf16)


def encoder_gradient(rows_ref, d_pre_ref, out_ref, bias_ref):
    rows = rows_ref[...]
    sums = []
    for n in range(4):
        pair = [d_pre_ref[:, q * 64 : (q + 1) * 64, :].reshape(512, 128) for q in (2 * n, 2 * n + 1)]
        sums += [jnp.sum(part.astype(f32), axis=0, keepdims=True) for part in pair]
        d_pre = jnp.concatenate(pair, axis=1)
        out_ref[:, n * 256 : (n + 1) * 256] = matmul(rows, d_pre, ((0,), (0,))).astype(bf16)
    bias_ref[...] = jnp.concatenate(sums, axis=0).astype(bf16)


def gradients(acts_ref, err_ref, w_ref, norms_ref, rows_ref, d_pre_ref, dec_far, dec_bias, enc_far, enc_bias, *own):
    dec_ref, enc_ref, dec_sem, enc_sem = own
    decoder_gradient(acts_ref, err_ref, w_ref, norms_ref, dec_ref, dec_bias)
    dec_out = pltpu.make_async_copy(dec_ref, dec_far, dec_sem)
    dec_out.start()
    encoder_gradient(rows_ref, d_pre_ref, enc_ref, enc_bias)
    enc_out = pltpu.make_async_copy(enc_ref, enc_far, enc_sem)
    enc_out.start()
    dec_out.wait()
    enc_out.wait()


def exchange(blocks, axes):
    return lax.all_to_all(blocks, axes, 0, 0, tiled=True)


def local(residual, w_enc, b_enc, w_dec, b_dec):
    w_across = w_dec.T
    work = 2 * 512 * 576 * 1024
    near, squares = call(spread_rows, [((256, 576), bf16), ((8, 128), f32)], residual, w_across)
    half = lax.axis_index("c").astype(jnp.int32).reshape(1)
    near, half = lax.optimization_barrier((near, half))
    near = exchange(near.reshape(32, 8, 576), CHIPS).reshape(256, 576)
    rows_all = lax.all_gather(near, "c", axis=0, tiled=True)
    sent = call(encode, [((8, 528, 128), bf16)], rows_all, w_enc, squares, flops=work)[0]
    acts, pre, norms, penalty = call(
        activate,
        [((8, 512, 128), bf16), ((512, 128), f32), ((8, 128), f32), ((1, 128), f32)],
        exchange(sent, LAYER),
        b_enc.reshape(8, 128),
    )
    acts = exchange(acts, LAYER)

    other, mine = call(
        decode, [((256, 576), bf16), ((256, 576), f32)], half, acts, w_across, flops=work, smem=(0,)
    )
    both = lax.all_gather(other, "c", axis=0, tiled=True)
    pair = call(add_pair, [((256, 576), bf16)], half, both, mine, smem=(0,))[0]
    recon = exchange(pair.reshape(32, 8, 576), CHIPS)
    packed = call(
        residue,
        [((256, 640), bf16)],
        recon.reshape(256, 576),
        b_dec,
        residual,
        penalty,
    )[0]
    packed = exchange(packed.reshape(32, 8, 640), CHIPS).reshape(256, 640)
    err = lax.all_gather(packed, "c", axis=0, tiled=True)

    sent = call(decode_back, [((8, 528, 128), bf16)], err, w_across, flops=work)[0]
    d_pre, loss = call(mask, [((8, 512, 128), bf16), ((1, 1), f32)], exchange(sent, LAYER), pre, norms)
    d_pre, loss = lax.optimization_barrier((d_pre, loss.reshape(())))
    weights, wide = ((576, 1024), bf16), pltpu.VMEM((576, 1024), bf16)
    grad_dec, grad_bdec, grad_enc, grad_benc = call(
        gradients,
        [weights, ((576,), bf16), weights, ((8, 128), bf16)],
        acts,
        err,
        w_across,
        norms,
        rows_all,
        exchange(d_pre, LAYER),
        flops=2 * work,
        far=(0, 2),
        scratch=(wide, wide, pltpu.SemaphoreType.DMA, pltpu.SemaphoreType.DMA),
    )
    return (
        grad_enc,
        grad_benc.reshape(1024),
        grad_dec.T,
        grad_bdec,
        loss,
    )


def solution(mesh):
    fine = Mesh(mesh.devices.reshape(4, 2, 8, 4, 2), ("x", "yl", "z", "yh", "c"))
    placed = (P(LATENT, LAYER), P(LAYER, LATENT), P(LATENT), P(LATENT, LAYER), P(LAYER))
    return jax.shard_map(
        local,
        mesh=fine,
        in_specs=placed,
        out_specs=(P(LAYER, LATENT), P(LATENT), P(LATENT, LAYER), P(LAYER), P()),
        check_vma=False,
    )
```

```python
import math

import jax
import jax.numpy as jnp
from jax import lax
from jax.experimental import pallas as pl
from jax.experimental.pallas import tpu as pltpu
from jax.sharding import Mesh, PartitionSpec as P

D = 4608
ROWS = 512
LAYER = ("x", "yl")
CHIPS = ("z", "yh")
LATENT = ("z", "yh", "c")
f32, bf16 = jnp.float32, jnp.bfloat16

penalty_weight = 0.5


def call(body, outs, *args, flops=0, smem=(), far=(), scratch=()):
    outs = [pltpu.HBM(*o) if i in far else jax.ShapeDtypeStruct(*o) for i, o in enumerate(outs)]
    size = sum(math.prod(a.shape) * jnp.dtype(a.dtype).itemsize for a in list(args) + outs)
    return pl.pallas_call(
        body,
        out_shape=outs,
        in_specs=[
            pl.BlockSpec(memory_space=pltpu.SMEM if i in smem else pltpu.VMEM) for i in range(len(args))
        ],
        out_specs=[pl.BlockSpec(memory_space=pltpu.HBM if i in far else pltpu.VMEM) for i in range(len(outs))],
        scratch_shapes=list(scratch),
        cost_estimate=pl.CostEstimate(flops=flops, bytes_accessed=size, transcendentals=0),
        compiler_params=pltpu.CompilerParams(vmem_limit_bytes=24 * 2**20),
    )(*args)


def matmul(a, b, dims):
    return lax.dot_general(a, b, (dims, ((), ())), preferred_element_type=f32)


def row_block(ref, lo, count):
    parts = [ref[pl.ds(lo, count), q * 64 : (q + 1) * 64, :].reshape(count * 64, 128) for q in range(8)]
    return jnp.concatenate(parts, axis=1)


STEPS = 252.0


def spread_rows(rows_ref, out_ref):
    rows = rows_ref[...].astype(f32)
    out_ref[...] = jnp.broadcast_to(rows[None], (32, 8, 576)).reshape(256, 576).astype(bf16)


def sum_squares(across_ref, _, squares_ref):
    for q in range(8):
        wide = across_ref[:, q * 128 : (q + 1) * 128].astype(f32)
        squares_ref[q : q + 1, :] = jnp.sum(wide * wide, axis=0, keepdims=True)


def encode(rows_ref, w_ref, squares_ref, sent_ref):
    rows = rows_ref[...]
    tops = []
    for n in range(4):
        part = matmul(rows, w_ref[:, n * 256 : (n + 1) * 256], ((1,), (0,))).reshape(8, 64, 256)
        size = jnp.abs(part)
        top = (jnp.max(size, axis=1, keepdims=True) * (1 + 2.0**-7) + 1e-30).astype(bf16).astype(f32)
        code = jnp.exp2(size * (STEPS / top) - 126.0)
        code = jnp.where(part < 0, -code, code).astype(bf16)
        for h in range(2):
            at = pl.ds((2 * n + h) * 64, 64)
            lanes = slice(h * 128, (h + 1) * 128)
            sent_ref[:, at, :] = code[:, :, lanes]
            tops.append(top[:, :, lanes])
    squares = jnp.broadcast_to(squares_ref[...][None], (8, 8, 128))
    sent_ref[:, 512:528, :] = jnp.concatenate([squares] + tops, axis=1).astype(bf16)


def activate(got_ref, bias_ref, acts_ref, pre_ref, norms_ref, penalty_ref):
    extra = got_ref[:, 512:528, :].astype(f32)
    norms = jnp.sqrt(jnp.sum(extra[:, :8, :], axis=0) + 1e-06)
    norms_ref[...] = norms
    penalty = jnp.zeros((1, 128), f32)
    for q in range(8):
        at = pl.ds(q * 64, 64)
        code = got_ref[:, at, :].astype(f32)
        part = (jnp.log2(jnp.abs(code)) + 126.0) * (extra[:, 8 + q : 9 + q, :] / STEPS)
        pre = jnp.sum(jnp.where(code < 0, -part, part), axis=0) + bias_ref[q : q + 1, :]
        pre_ref[at, :] = pre
        acts = jnp.maximum(pre, 0.0).astype(bf16)
        acts_ref[:, at, :] = jnp.broadcast_to(acts[None], (8, 64, 128))
        penalty = penalty + jnp.sum(acts.astype(f32), axis=0, keepdims=True) * norms[q : q + 1, :]
    penalty_ref[...] = penalty_weight * penalty


def decode(half_ref, acts_ref, w_ref, other_ref, mine_ref):
    for half, ref in ((1 - half_ref[0], other_ref), (half_ref[0], mine_ref)):
        acts = row_block(acts_ref, half * 4, 4)
        ref[...] = matmul(acts, w_ref[...], ((1,), (1,))).astype(ref.dtype)


def add_pair(half_ref, both_ref, mine_ref, out_ref):
    other = both_ref[pl.ds(pl.multiple_of((1 - half_ref[0]) * 256, 256), 256), :]
    out_ref[...] = (mine_ref[...] + other.astype(f32)).astype(bf16)


def residue(got_ref, bias_ref, residual_ref, penalty_ref, out_ref):
    recon = jnp.sum(got_ref[...].astype(f32).reshape(32, 8, 576), axis=0) + bias_ref[...][None, :]
    err = recon - residual_ref[...].astype(f32)
    total = jnp.sum(err * err, axis=(0, 1), keepdims=True) + jnp.sum(penalty_ref[...], axis=(0, 1), keepdims=True)
    high = total.astype(bf16).astype(f32)
    row = lax.broadcasted_iota(jnp.int32, (8, 64), 0)
    lane = lax.broadcasted_iota(jnp.int32, (8, 64), 1)
    tail = jnp.where(row == 0, jnp.where(lane == 0, high, jnp.where(lane == 1, total - high, 0.0)), 0.0)
    block = jnp.concatenate([err / 8.0, tail], axis=1)
    out_ref[...] = jnp.broadcast_to(block[None], (32, 8, 640)).reshape(256, 640).astype(bf16)


def decode_back(err_ref, w_ref, sent_ref):
    err = err_ref[:, :576]
    lane = lax.broadcasted_iota(jnp.int32, (512, 128), 1)
    tail = jnp.where(lane >= 64, err_ref[:, 512:640].astype(f32), 0.0)
    total = jnp.sum(tail, axis=(0, 1), keepdims=True)
    high = total.astype(bf16).astype(f32)
    row = lax.broadcasted_iota(jnp.int32, (16, 128), 0)
    lane = lax.broadcasted_iota(jnp.int32, (16, 128), 1)
    tail = jnp.where(row == 0, jnp.where(lane == 0, high, jnp.where(lane == 1, total - high, 0.0)), 0.0)
    sent_ref[:, 512:528, :] = jnp.broadcast_to(tail.astype(bf16)[None], (8, 16, 128))
    for n in range(4):
        part = matmul(err, w_ref[:, n * 256 : (n + 1) * 256], ((1,), (0,))).astype(bf16)
        for h in range(2):
            at = pl.ds((2 * n + h) * 64, 64)
            sent_ref[:, at, :] = part[:, h * 128 : (h + 1) * 128].reshape(8, 64, 128)


def mask(got_ref, pre_ref, norms_ref, out_ref, loss_ref):
    for q in range(8):
        at = pl.ds(q * 64, 64)
        d_acts = jnp.sum(got_ref[:, at, :].astype(f32), axis=0)
        d_acts = d_acts + penalty_weight / 16.0 * norms_ref[q : q + 1, :]
        d_pre = jnp.where(pre_ref[at, :] > 0, d_acts, 0.0).astype(bf16)
        out_ref[:, at, :] = jnp.broadcast_to(d_pre[None], (8, 64, 128))
    total = jnp.sum(got_ref[:, 512:528, :].astype(f32), axis=0)
    loss_ref[...] = jnp.sum(total, axis=(0, 1), keepdims=True) / (ROWS * D)


def decoder_gradient(acts_ref, err_ref, w_ref, norms_ref, out_ref, bias_ref):
    err = err_ref[:, :576]
    bias_ref[...] = jnp.sum(err.astype(f32), axis=0).astype(bf16)
    for n in range(4):
        at = slice(n * 256, (n + 1) * 256)
        acts = jnp.concatenate(
            [acts_ref[:, q * 64 : (q + 1) * 64, :].reshape(512, 128) for q in (2 * n, 2 * n + 1)], axis=1
        )
        norms = jnp.concatenate([norms_ref[q : q + 1, :] for q in (2 * n, 2 * n + 1)], axis=1)
        scale = penalty_weight / 16.0 * jnp.sum(acts.astype(f32), axis=0, keepdims=True) / norms
        outer = matmul(err, acts, ((0,), (0,)))
        out_ref[:, at] = (outer + scale * w_ref[:, at].astype(f32)).astype(bf16)


def encoder_gradient(rows_ref, d_pre_ref, out_ref, bias_ref):
    rows = rows_ref[...]
    sums = []
    for n in range(4):
        pair = [d_pre_ref[:, q * 64 : (q + 1) * 64, :].reshape(512, 128) for q in (2 * n, 2 * n + 1)]
        sums += [jnp.sum(part.astype(f32), axis=0, keepdims=True) for part in pair]
        d_pre = jnp.concatenate(pair, axis=1)
        out_ref[:, n * 256 : (n + 1) * 256] = matmul(rows, d_pre, ((0,), (0,))).astype(bf16)
    bias_ref[...] = jnp.concatenate(sums, axis=0).astype(bf16)


def gradients(acts_ref, err_ref, w_ref, norms_ref, rows_ref, d_pre_ref, dec_far, dec_bias, enc_far, enc_bias, *own):
    dec_ref, enc_ref, dec_sem, enc_sem = own
    decoder_gradient(acts_ref, err_ref, w_ref, norms_ref, dec_ref, dec_bias)
    dec_out = pltpu.make_async_copy(dec_ref, dec_far, dec_sem)
    dec_out.start()
    encoder_gradient(rows_ref, d_pre_ref, enc_ref, enc_bias)
    enc_out = pltpu.make_async_copy(enc_ref, enc_far, enc_sem)
    enc_out.start()
    dec_out.wait()
    enc_out.wait()


def exchange(blocks, axes):
    return lax.all_to_all(blocks, axes, 0, 0, tiled=True)


def local(residual, w_enc, b_enc, w_dec, b_dec):
    w_across = w_dec.T
    work = 2 * 512 * 576 * 1024
    near = call(spread_rows, [((256, 576), bf16)], residual)[0]
    half = lax.axis_index("c").astype(jnp.int32).reshape(1)
    near, half = lax.optimization_barrier((near, half))
    near = exchange(near.reshape(32, 8, 576), CHIPS)
    rows_all = lax.all_gather(near.reshape(256, 576), "c", axis=0, tiled=True)
    squares = call(sum_squares, [((8, 128), f32)], w_across, rows_all)[0]
    sent = call(encode, [((8, 528, 128), bf16)], rows_all, w_enc, squares, flops=work)[0]
    acts, pre, norms, penalty = call(
        activate,
        [((8, 512, 128), bf16), ((512, 128), f32), ((8, 128), f32), ((1, 128), f32)],
        exchange(sent, LAYER),
        b_enc.reshape(8, 128),
    )
    acts = exchange(acts, LAYER)

    other, mine = call(
        decode, [((256, 576), bf16), ((256, 576), f32)], half, acts, w_across, flops=work, smem=(0,)
    )
    both = lax.all_gather(other, "c", axis=0, tiled=True)
    pair = call(add_pair, [((256, 576), bf16)], half, both, mine, smem=(0,))[0]
    recon = exchange(pair.reshape(32, 8, 576), CHIPS)
    packed = call(
        residue,
        [((256, 640), bf16)],
        recon.reshape(256, 576),
        b_dec,
        residual,
        penalty,
    )[0]
    packed = exchange(packed.reshape(32, 8, 640), CHIPS).reshape(256, 640)
    err = lax.all_gather(packed, "c", axis=0, tiled=True)

    sent = call(decode_back, [((8, 528, 128), bf16)], err, w_across, flops=work)[0]
    d_pre, loss = call(mask, [((8, 512, 128), bf16), ((1, 1), f32)], exchange(sent, LAYER), pre, norms)
    d_pre, loss = lax.optimization_barrier((d_pre, loss.reshape(())))
    weights, wide = ((576, 1024), bf16), pltpu.VMEM((576, 1024), bf16)
    grad_dec, grad_bdec, grad_enc, grad_benc = call(
        gradients,
        [weights, ((576,), bf16), weights, ((8, 128), bf16)],
        acts,
        err,
        w_across,
        norms,
        rows_all,
        exchange(d_pre, LAYER),
        flops=2 * work,
        far=(0, 2),
        scratch=(wide, wide, pltpu.SemaphoreType.DMA, pltpu.SemaphoreType.DMA),
    )
    return (
        grad_enc,
        grad_benc.reshape(1024),
        grad_dec.T,
        grad_bdec,
        loss,
    )


def solution(mesh):
    fine = Mesh(mesh.devices.reshape(4, 2, 8, 4, 2), ("x", "yl", "z", "yh", "c"))
    placed = (P(LATENT, LAYER), P(LAYER, LATENT), P(LATENT), P(LATENT, LAYER), P(LAYER))
    return jax.shard_map(
        local,
        mesh=fine,
        in_specs=placed,
        out_specs=(P(LAYER, LATENT), P(LATENT), P(LATENT, LAYER), P(LAYER), P()),
        check_vma=False,
    )
```

```python
import math

import jax
import jax.numpy as jnp
from jax import lax
from jax.experimental import pallas as pl
from jax.experimental.pallas import tpu as pltpu
from jax.sharding import Mesh, PartitionSpec as P

D = 4608
ROWS = 512
LAYER = ("x", "yl")
CHIPS = ("z", "yh")
LATENT = ("z", "yh", "c")
f32, bf16 = jnp.float32, jnp.bfloat16

penalty_weight = 0.5


def call(body, outs, *args, flops=0, smem=(), far=(), scratch=()):
    outs = [pltpu.HBM(*o) if i in far else jax.ShapeDtypeStruct(*o) for i, o in enumerate(outs)]
    size = sum(math.prod(a.shape) * jnp.dtype(a.dtype).itemsize for a in list(args) + outs)
    return pl.pallas_call(
        body,
        out_shape=outs,
        in_specs=[
            pl.BlockSpec(memory_space=pltpu.SMEM if i in smem else pltpu.VMEM) for i in range(len(args))
        ],
        out_specs=[pl.BlockSpec(memory_space=pltpu.HBM if i in far else pltpu.VMEM) for i in range(len(outs))],
        scratch_shapes=list(scratch),
        cost_estimate=pl.CostEstimate(flops=flops, bytes_accessed=size, transcendentals=0),
        compiler_params=pltpu.CompilerParams(vmem_limit_bytes=24 * 2**20),
    )(*args)


def matmul(a, b, dims):
    return lax.dot_general(a, b, (dims, ((), ())), preferred_element_type=f32)


def row_block(ref, lo, count):
    parts = [ref[pl.ds(lo, count), q * 64 : (q + 1) * 64, :].reshape(count * 64, 128) for q in range(8)]
    return jnp.concatenate(parts, axis=1)


STEPS, LEAST = 250.0, -124.0


def spread_rows(rows_ref, out_ref):
    rows = rows_ref[...].astype(f32)
    out_ref[...] = jnp.broadcast_to(rows[None], (32, 8, 576)).reshape(256, 576).astype(bf16)


def sum_squares(across_ref, _, squares_ref):
    for q in range(8):
        wide = across_ref[:, q * 128 : (q + 1) * 128].astype(f32)
        squares_ref[q : q + 1, :] = jnp.sum(wide * wide, axis=0, keepdims=True)


def encode(rows_ref, w_ref, squares_ref, sent_ref):
    rows = rows_ref[...]
    tops = []
    for n in range(4):
        part = matmul(rows, w_ref[:, n * 256 : (n + 1) * 256], ((1,), (0,))).reshape(8, 64, 256)
        size = jnp.abs(part)
        top = (jnp.max(size, axis=1, keepdims=True) * (1 + 2.0**-7) + 1e-30).astype(bf16).astype(f32)
        code = jnp.exp2(size * (STEPS / top) + LEAST)
        code = jnp.where(part < 0, -code, code).astype(bf16)
        for h in range(2):
            at = pl.ds((2 * n + h) * 64, 64)
            lanes = slice(h * 128, (h + 1) * 128)
            sent_ref[:, at, :] = code[:, :, lanes]
            tops.append(top[:, :, lanes])
    squares = jnp.broadcast_to(squares_ref[...][None], (8, 8, 128))
    sent_ref[:, 512:528, :] = jnp.concatenate([squares] + tops, axis=1).astype(bf16)


def activate(got_ref, bias_ref, acts_ref, pre_ref, norms_ref, penalty_ref):
    extra = got_ref[:, 512:528, :].astype(f32)
    norms = jnp.sqrt(jnp.sum(extra[:, :8, :], axis=0) + 1e-06)
    norms_ref[...] = norms
    penalty = jnp.zeros((1, 128), f32)
    for q in range(8):
        at = pl.ds(q * 64, 64)
        code = got_ref[:, at, :].astype(f32)
        part = (jnp.log2(jnp.abs(code)) - LEAST) * (extra[:, 8 + q : 9 + q, :] / STEPS)
        pre = jnp.sum(jnp.where(code < 0, -part, part), axis=0) + bias_ref[q : q + 1, :]
        pre_ref[at, :] = pre
        acts = jnp.maximum(pre, 0.0).astype(bf16)
        acts_ref[:, at, :] = jnp.broadcast_to(acts[None], (8, 64, 128))
        penalty = penalty + jnp.sum(acts.astype(f32), axis=0, keepdims=True) * norms[q : q + 1, :]
    penalty_ref[...] = penalty_weight * penalty


def decode(half_ref, acts_ref, w_ref, other_ref, mine_ref):
    for half, ref in ((1 - half_ref[0], other_ref), (half_ref[0], mine_ref)):
        acts = row_block(acts_ref, half * 4, 4)
        ref[...] = matmul(acts, w_ref[...], ((1,), (1,))).astype(ref.dtype)


def add_pair(half_ref, both_ref, mine_ref, out_ref):
    other = both_ref[pl.ds(pl.multiple_of((1 - half_ref[0]) * 256, 256), 256), :]
    out_ref[...] = (mine_ref[...] + other.astype(f32)).astype(bf16)


def residue(got_ref, bias_ref, residual_ref, penalty_ref, out_ref):
    recon = jnp.sum(got_ref[...].astype(f32).reshape(32, 8, 576), axis=0) + bias_ref[...][None, :]
    err = recon - residual_ref[...].astype(f32)
    total = jnp.sum(err * err, axis=(0, 1), keepdims=True) + jnp.sum(penalty_ref[...], axis=(0, 1), keepdims=True)
    high = total.astype(bf16).astype(f32)
    row = lax.broadcasted_iota(jnp.int32, (8, 64), 0)
    lane = lax.broadcasted_iota(jnp.int32, (8, 64), 1)
    tail = jnp.where(row == 0, jnp.where(lane == 0, high, jnp.where(lane == 1, total - high, 0.0)), 0.0)
    block = jnp.concatenate([err / 8.0, tail], axis=1)
    out_ref[...] = jnp.broadcast_to(block[None], (32, 8, 640)).reshape(256, 640).astype(bf16)


def decode_back(err_ref, w_ref, sent_ref):
    err = err_ref[:, :576]
    lane = lax.broadcasted_iota(jnp.int32, (512, 128), 1)
    tail = jnp.where(lane >= 64, err_ref[:, 512:640].astype(f32), 0.0)
    total = jnp.sum(tail, axis=(0, 1), keepdims=True)
    high = total.astype(bf16).astype(f32)
    row = lax.broadcasted_iota(jnp.int32, (16, 128), 0)
    lane = lax.broadcasted_iota(jnp.int32, (16, 128), 1)
    tail = jnp.where(row == 0, jnp.where(lane == 0, high, jnp.where(lane == 1, total - high, 0.0)), 0.0)
    sent_ref[:, 512:528, :] = jnp.broadcast_to(tail.astype(bf16)[None], (8, 16, 128))
    for n in range(4):
        part = matmul(err, w_ref[:, n * 256 : (n + 1) * 256], ((1,), (0,))).astype(bf16)
        for h in range(2):
            at = pl.ds((2 * n + h) * 64, 64)
            sent_ref[:, at, :] = part[:, h * 128 : (h + 1) * 128].reshape(8, 64, 128)


def mask(got_ref, pre_ref, norms_ref, out_ref, loss_ref):
    for q in range(8):
        at = pl.ds(q * 64, 64)
        d_acts = jnp.sum(got_ref[:, at, :].astype(f32), axis=0)
        d_acts = d_acts + penalty_weight / 16.0 * norms_ref[q : q + 1, :]
        d_pre = jnp.where(pre_ref[at, :] > 0, d_acts, 0.0).astype(bf16)
        out_ref[:, at, :] = jnp.broadcast_to(d_pre[None], (8, 64, 128))
    total = jnp.sum(got_ref[:, 512:528, :].astype(f32), axis=0)
    loss_ref[...] = jnp.sum(total, axis=(0, 1), keepdims=True) / (ROWS * D)


def decoder_gradient(acts_ref, err_ref, w_ref, norms_ref, out_ref, bias_ref):
    err = err_ref[:, :576]
    bias_ref[...] = jnp.sum(err.astype(f32), axis=0).astype(bf16)
    for n in range(4):
        at = slice(n * 256, (n + 1) * 256)
        acts = jnp.concatenate(
            [acts_ref[:, q * 64 : (q + 1) * 64, :].reshape(512, 128) for q in (2 * n, 2 * n + 1)], axis=1
        )
        norms = jnp.concatenate([norms_ref[q : q + 1, :] for q in (2 * n, 2 * n + 1)], axis=1)
        scale = penalty_weight / 16.0 * jnp.sum(acts.astype(f32), axis=0, keepdims=True) / norms
        outer = matmul(err, acts, ((0,), (0,)))
        out_ref[:, at] = (outer + scale * w_ref[:, at].astype(f32)).astype(bf16)


def encoder_gradient(rows_ref, d_pre_ref, out_ref, bias_ref):
    rows = rows_ref[...]
    sums = []
    for n in range(4):
        pair = [d_pre_ref[:, q * 64 : (q + 1) * 64, :].reshape(512, 128) for q in (2 * n, 2 * n + 1)]
        sums += [jnp.sum(part.astype(f32), axis=0, keepdims=True) for part in pair]
        d_pre = jnp.concatenate(pair, axis=1)
        out_ref[:, n * 256 : (n + 1) * 256] = matmul(rows, d_pre, ((0,), (0,))).astype(bf16)
    bias_ref[...] = jnp.concatenate(sums, axis=0).astype(bf16)


def gradients(acts_ref, err_ref, w_ref, norms_ref, rows_ref, d_pre_ref, dec_far, dec_bias, enc_far, enc_bias, *own):
    dec_ref, enc_ref, dec_sem, enc_sem = own
    decoder_gradient(acts_ref, err_ref, w_ref, norms_ref, dec_ref, dec_bias)
    dec_out = pltpu.make_async_copy(dec_ref, dec_far, dec_sem)
    dec_out.start()
    encoder_gradient(rows_ref, d_pre_ref, enc_ref, enc_bias)
    enc_out = pltpu.make_async_copy(enc_ref, enc_far, enc_sem)
    enc_out.start()
    dec_out.wait()
    enc_out.wait()


def exchange(blocks, axes):
    return lax.all_to_all(blocks, axes, 0, 0, tiled=True)


def local(residual, w_enc, b_enc, w_dec, b_dec):
    w_across = w_dec.T
    work = 2 * 512 * 576 * 1024
    near = call(spread_rows, [((256, 576), bf16)], residual)[0]
    half = lax.axis_index("c").astype(jnp.int32).reshape(1)
    near, half = lax.optimization_barrier((near, half))
    near = exchange(near.reshape(32, 8, 576), CHIPS)
    rows_all = lax.all_gather(near.reshape(256, 576), "c", axis=0, tiled=True)
    squares = call(sum_squares, [((8, 128), f32)], w_across, rows_all)[0]
    sent = call(encode, [((8, 528, 128), bf16)], rows_all, w_enc, squares, flops=work)[0]
    acts, pre, norms, penalty = call(
        activate,
        [((8, 512, 128), bf16), ((512, 128), f32), ((8, 128), f32), ((1, 128), f32)],
        exchange(sent, LAYER),
        b_enc.reshape(8, 128),
    )
    acts = exchange(acts, LAYER)

    other, mine = call(
        decode, [((256, 576), bf16), ((256, 576), f32)], half, acts, w_across, flops=work, smem=(0,)
    )
    both = lax.all_gather(other, "c", axis=0, tiled=True)
    pair = call(add_pair, [((256, 576), bf16)], half, both, mine, smem=(0,))[0]
    recon = exchange(pair.reshape(32, 8, 576), CHIPS)
    packed = call(
        residue,
        [((256, 640), bf16)],
        recon.reshape(256, 576),
        b_dec,
        residual,
        penalty,
    )[0]
    packed = exchange(packed.reshape(32, 8, 640), CHIPS).reshape(256, 640)
    err = lax.all_gather(packed, "c", axis=0, tiled=True)

    sent = call(decode_back, [((8, 528, 128), bf16)], err, w_across, flops=work)[0]
    d_pre, loss = call(mask, [((8, 512, 128), bf16), ((1, 1), f32)], exchange(sent, LAYER), pre, norms)
    d_pre, loss = lax.optimization_barrier((d_pre, loss.reshape(())))
    weights, wide = ((576, 1024), bf16), pltpu.VMEM((576, 1024), bf16)
    grad_dec, grad_bdec, grad_enc, grad_benc = call(
        gradients,
        [weights, ((576,), bf16), weights, ((8, 128), bf16)],
        acts,
        err,
        w_across,
        norms,
        rows_all,
        exchange(d_pre, LAYER),
        flops=2 * work,
        far=(0, 2),
        scratch=(wide, wide, pltpu.SemaphoreType.DMA, pltpu.SemaphoreType.DMA),
    )
    return (
        grad_enc,
        grad_benc.reshape(1024),
        grad_dec.T,
        grad_bdec,
        loss,
    )


def solution(mesh):
    fine = Mesh(mesh.devices.reshape(4, 2, 8, 4, 2), ("x", "yl", "z", "yh", "c"))
    placed = (P(LATENT, LAYER), P(LAYER, LATENT), P(LATENT), P(LATENT, LAYER), P(LAYER))
    return jax.shard_map(
        local,
        mesh=fine,
        in_specs=placed,
        out_specs=(P(LAYER, LATENT), P(LATENT), P(LATENT, LAYER), P(LAYER), P()),
        check_vma=False,
    )
```

```python
import math

import jax
import jax.numpy as jnp
from jax import lax
from jax.experimental import pallas as pl
from jax.experimental.pallas import tpu as pltpu
from jax.sharding import Mesh, PartitionSpec as P

D = 4608
ROWS = 512
LAYER = ("x", "yl")
CHIPS = ("z", "yh")
LATENT = ("z", "yh", "c")
f32, bf16 = jnp.float32, jnp.bfloat16

penalty_weight = 0.5


def call(body, outs, *args, flops=0, smem=(), far=(), scratch=()):
    outs = [pltpu.HBM(*o) if i in far else jax.ShapeDtypeStruct(*o) for i, o in enumerate(outs)]
    size = sum(math.prod(a.shape) * jnp.dtype(a.dtype).itemsize for a in list(args) + outs)
    return pl.pallas_call(
        body,
        out_shape=outs,
        in_specs=[
            pl.BlockSpec(memory_space=pltpu.SMEM if i in smem else pltpu.VMEM) for i in range(len(args))
        ],
        out_specs=[pl.BlockSpec(memory_space=pltpu.HBM if i in far else pltpu.VMEM) for i in range(len(outs))],
        scratch_shapes=list(scratch),
        cost_estimate=pl.CostEstimate(flops=flops, bytes_accessed=size, transcendentals=0),
        compiler_params=pltpu.CompilerParams(vmem_limit_bytes=24 * 2**20),
    )(*args)


def matmul(a, b, dims):
    return lax.dot_general(a, b, (dims, ((), ())), preferred_element_type=f32)


def row_block(ref, lo, count):
    parts = [ref[pl.ds(lo, count), q * 64 : (q + 1) * 64, :].reshape(count * 64, 128) for q in range(8)]
    return jnp.concatenate(parts, axis=1)


STEPS, LEAST = 250.0, -124.0


def spread_rows(rows_ref, out_ref):
    rows = rows_ref[...].astype(f32)
    out_ref[...] = jnp.broadcast_to(rows[None], (32, 8, 576)).reshape(256, 576).astype(bf16)


def sum_squares(across_ref, _, squares_ref):
    for q in range(8):
        wide = across_ref[:, q * 128 : (q + 1) * 128].astype(f32)
        squares_ref[q : q + 1, :] = jnp.sum(wide * wide, axis=0, keepdims=True)


def encode(rows_ref, w_ref, squares_ref, sent_ref):
    rows = rows_ref[...]
    tops = []
    for n in range(4):
        part = matmul(rows, w_ref[:, n * 256 : (n + 1) * 256], ((1,), (0,))).reshape(8, 64, 256)
        size = jnp.abs(part)
        top = (jnp.max(size, axis=1, keepdims=True) * (1 + 2.0**-7) + 1e-30).astype(bf16).astype(f32)
        code = jnp.exp2(size * (STEPS / top) + LEAST)
        code = jnp.where(part < 0, -code, code).astype(bf16)
        for h in range(2):
            at = pl.ds((2 * n + h) * 64, 64)
            lanes = slice(h * 128, (h + 1) * 128)
            sent_ref[:, at, :] = code[:, :, lanes]
            tops.append(top[:, :, lanes])
    squares = jnp.broadcast_to(squares_ref[...][None], (8, 8, 128))
    sent_ref[:, 512:528, :] = jnp.concatenate([squares] + tops, axis=1).astype(bf16)


def activate(got_ref, bias_ref, acts_ref, pre_ref, norms_ref, penalty_ref):
    extra = got_ref[:, 512:528, :].astype(f32)
    norms = jnp.sqrt(jnp.sum(extra[:, :8, :], axis=0) + 1e-06)
    norms_ref[...] = norms
    penalty = jnp.zeros((1, 128), f32)
    for q in range(8):
        at = pl.ds(q * 64, 64)
        code = got_ref[:, at, :].astype(f32)
        part = (jnp.log2(jnp.abs(code)) - LEAST) * (extra[:, 8 + q : 9 + q, :] / STEPS)
        pre = jnp.sum(jnp.where(code < 0, -part, part), axis=0) + bias_ref[q : q + 1, :]
        pre_ref[at, :] = pre
        acts = jnp.maximum(pre, 0.0).astype(bf16)
        acts_ref[:, at, :] = jnp.broadcast_to(acts[None], (8, 64, 128))
        penalty = penalty + jnp.sum(acts.astype(f32), axis=0, keepdims=True) * norms[q : q + 1, :]
    penalty_ref[...] = penalty_weight * penalty


def decode(half_ref, acts_ref, w_ref, other_ref, mine_ref):
    for half, ref in ((1 - half_ref[0], other_ref), (half_ref[0], mine_ref)):
        acts = row_block(acts_ref, half * 4, 4)
        ref[...] = matmul(acts, w_ref[...], ((1,), (1,))).astype(ref.dtype)


def add_pair(half_ref, both_ref, mine_ref, out_ref):
    other = both_ref[pl.ds(pl.multiple_of((1 - half_ref[0]) * 256, 256), 256), :]
    out_ref[...] = (mine_ref[...] + other.astype(f32)).astype(bf16)


def residue(got_ref, bias_ref, residual_ref, penalty_ref, out_ref):
    recon = jnp.sum(got_ref[...].astype(f32).reshape(32, 8, 576), axis=0) + bias_ref[...][None, :]
    err = recon - residual_ref[...].astype(f32)
    total = jnp.sum(err * err, axis=(0, 1), keepdims=True) + jnp.sum(penalty_ref[...], axis=(0, 1), keepdims=True)
    high = total.astype(bf16).astype(f32)
    row = lax.broadcasted_iota(jnp.int32, (8, 64), 0)
    lane = lax.broadcasted_iota(jnp.int32, (8, 64), 1)
    tail = jnp.where(row == 0, jnp.where(lane == 0, high, jnp.where(lane == 1, total - high, 0.0)), 0.0)
    block = jnp.concatenate([err / 8.0, tail], axis=1)
    out_ref[...] = jnp.broadcast_to(block[None], (32, 8, 640)).reshape(256, 640).astype(bf16)


def decode_back(err_ref, w_ref, sent_ref):
    err = err_ref[:, :576]
    lane = lax.broadcasted_iota(jnp.int32, (512, 128), 1)
    tail = jnp.where(lane >= 64, err_ref[:, 512:640].astype(f32), 0.0)
    total = jnp.sum(tail, axis=(0, 1), keepdims=True)
    high = total.astype(bf16).astype(f32)
    row = lax.broadcasted_iota(jnp.int32, (16, 128), 0)
    lane = lax.broadcasted_iota(jnp.int32, (16, 128), 1)
    tail = jnp.where(row == 0, jnp.where(lane == 0, high, jnp.where(lane == 1, total - high, 0.0)), 0.0)
    sent_ref[:, 512:528, :] = jnp.broadcast_to(tail.astype(bf16)[None], (8, 16, 128))
    for n in range(4):
        part = matmul(err, w_ref[:, n * 256 : (n + 1) * 256], ((1,), (0,))).astype(bf16)
        for h in range(2):
            at = pl.ds((2 * n + h) * 64, 64)
            sent_ref[:, at, :] = part[:, h * 128 : (h + 1) * 128].reshape(8, 64, 128)


def mask(got_ref, pre_ref, norms_ref, out_ref, loss_ref):
    for q in range(8):
        at = pl.ds(q * 64, 64)
        d_acts = jnp.sum(got_ref[:, at, :].astype(f32), axis=0)
        d_acts = d_acts + penalty_weight / 16.0 * norms_ref[q : q + 1, :]
        d_pre = jnp.where(pre_ref[at, :] > 0, d_acts, 0.0).astype(bf16)
        out_ref[:, at, :] = jnp.broadcast_to(d_pre[None], (8, 64, 128))
    total = jnp.sum(got_ref[:, 512:528, :].astype(f32), axis=0)
    loss_ref[...] = jnp.sum(total, axis=(0, 1), keepdims=True) / (ROWS * D)


def decoder_gradient(acts_ref, err_ref, w_ref, norms_ref, out_ref, bias_ref):
    err = err_ref[:, :576]
    bias_ref[...] = jnp.sum(err.astype(f32), axis=0).astype(bf16)
    for n in range(4):
        at = slice(n * 256, (n + 1) * 256)
        acts = jnp.concatenate(
            [acts_ref[:, q * 64 : (q + 1) * 64, :].reshape(512, 128) for q in (2 * n, 2 * n + 1)], axis=1
        )
        norms = jnp.concatenate([norms_ref[q : q + 1, :] for q in (2 * n, 2 * n + 1)], axis=1)
        scale = penalty_weight / 16.0 * jnp.sum(acts.astype(f32), axis=0, keepdims=True) / norms
        outer = matmul(err, acts, ((0,), (0,)))
        out_ref[:, at] = (outer + scale * w_ref[:, at].astype(f32)).astype(bf16)


def encoder_gradient(rows_ref, d_pre_ref, out_ref, bias_ref, halves):
    rows = rows_ref[...]
    sums = []
    for n in range(4):
        pair = [d_pre_ref[:, q * 64 : (q + 1) * 64, :].reshape(512, 128) for q in (2 * n, 2 * n + 1)]
        sums += [jnp.sum(part.astype(f32), axis=0, keepdims=True) for part in pair]
        d_pre = jnp.concatenate(pair, axis=1)
        out_ref[:, n * 256 : (n + 1) * 256] = matmul(rows, d_pre, ((0,), (0,))).astype(bf16)
        if n % 2:
            halves[n // 2].start()
    bias_ref[...] = jnp.concatenate(sums, axis=0).astype(bf16)


def gradients(acts_ref, err_ref, w_ref, norms_ref, rows_ref, d_pre_ref, dec_far, dec_bias, enc_far, enc_bias, *own):
    dec_ref, enc_ref, dec_sem, enc_sem = own
    decoder_gradient(acts_ref, err_ref, w_ref, norms_ref, dec_ref, dec_bias)
    dec_out = pltpu.make_async_copy(dec_ref, dec_far, dec_sem)
    dec_out.start()
    halves = [(slice(None), pl.ds(h * 512, 512)) for h in range(2)]
    enc_out = [pltpu.make_async_copy(enc_ref.at[at], enc_far.at[at], enc_sem.at[h]) for h, at in enumerate(halves)]
    encoder_gradient(rows_ref, d_pre_ref, enc_ref, enc_bias, enc_out)
    dec_out.wait()
    for copy in enc_out:
        copy.wait()


def exchange(blocks, axes):
    return lax.all_to_all(blocks, axes, 0, 0, tiled=True)


def local(residual, w_enc, b_enc, w_dec, b_dec):
    w_across = w_dec.T
    work = 2 * 512 * 576 * 1024
    near = call(spread_rows, [((256, 576), bf16)], residual)[0]
    half = lax.axis_index("c").astype(jnp.int32).reshape(1)
    near, half = lax.optimization_barrier((near, half))
    near = exchange(near.reshape(32, 8, 576), CHIPS)
    rows_all = lax.all_gather(near.reshape(256, 576), "c", axis=0, tiled=True)
    squares = call(sum_squares, [((8, 128), f32)], w_across, rows_all)[0]
    sent = call(encode, [((8, 528, 128), bf16)], rows_all, w_enc, squares, flops=work)[0]
    acts, pre, norms, penalty = call(
        activate,
        [((8, 512, 128), bf16), ((512, 128), f32), ((8, 128), f32), ((1, 128), f32)],
        exchange(sent, LAYER),
        b_enc.reshape(8, 128),
    )
    acts = exchange(acts, LAYER)

    other, mine = call(
        decode, [((256, 576), bf16), ((256, 576), f32)], half, acts, w_across, flops=work, smem=(0,)
    )
    both = lax.all_gather(other, "c", axis=0, tiled=True)
    pair = call(add_pair, [((256, 576), bf16)], half, both, mine, smem=(0,))[0]
    recon = exchange(pair.reshape(32, 8, 576), CHIPS)
    packed = call(
        residue,
        [((256, 640), bf16)],
        recon.reshape(256, 576),
        b_dec,
        residual,
        penalty,
    )[0]
    packed = exchange(packed.reshape(32, 8, 640), CHIPS).reshape(256, 640)
    err = lax.all_gather(packed, "c", axis=0, tiled=True)

    sent = call(decode_back, [((8, 528, 128), bf16)], err, w_across, flops=work)[0]
    d_pre, loss = call(mask, [((8, 512, 128), bf16), ((1, 1), f32)], exchange(sent, LAYER), pre, norms)
    d_pre, loss = lax.optimization_barrier((d_pre, loss.reshape(())))
    weights, wide = ((576, 1024), bf16), pltpu.VMEM((576, 1024), bf16)
    grad_dec, grad_bdec, grad_enc, grad_benc = call(
        gradients,
        [weights, ((576,), bf16), weights, ((8, 128), bf16)],
        acts,
        err,
        w_across,
        norms,
        rows_all,
        exchange(d_pre, LAYER),
        flops=2 * work,
        far=(0, 2),
        scratch=(wide, wide, pltpu.SemaphoreType.DMA, pltpu.SemaphoreType.DMA((2,))),
    )
    return (
        grad_enc,
        grad_benc.reshape(1024),
        grad_dec.T,
        grad_bdec,
        loss,
    )


def solution(mesh):
    fine = Mesh(mesh.devices.reshape(4, 2, 8, 4, 2), ("x", "yl", "z", "yh", "c"))
    placed = (P(LATENT, LAYER), P(LAYER, LATENT), P(LATENT), P(LATENT, LAYER), P(LAYER))
    return jax.shard_map(
        local,
        mesh=fine,
        in_specs=placed,
        out_specs=(P(LAYER, LATENT), P(LATENT), P(LATENT, LAYER), P(LAYER), P()),
        check_vma=False,
    )
```
